256 devices in a mesh: sample: 2 (over core), outer: 2 (over y_hi), inner: 64 (over y_lo, z, x).
Axes of the slice: x: 4, y: 4 (y_hi: 2, y_lo: 2; y = y_hi * 2 + y_lo), z: 8, core: 2. Of those that a mesh axis runs over, the one named last changes fastest.
Arguments:
- out_cotangent: bfloat16 [256, 384, 1152], P(('sample', 'outer', 'inner')), parts along dimension 0, may hold values from -6 to 6
- wo_spatial: bfloat16 [576, 1152], replicated, may hold values from -0.75 to 0.75
- wqkv_spatial: bfloat16 [1152, 1728], replicated, may hold values from -0.1875 to 0.1875
- wo_temporal: bfloat16 [576, 1152], replicated, may hold values from -0.75 to 0.75
- q_spatial: bfloat16 [256, 384, 576], P(('sample', 'outer', 'inner')), parts along dimension 0, may hold values from -6 to 6
- k_spatial: bfloat16 [256, 384, 576], P(('sample', 'outer', 'inner')), parts along dimension 0, may hold values from -6 to 6
- v_spatial: bfloat16 [256, 384, 576], P(('sample', 'outer', 'inner')), parts along dimension 0, may hold values from -6 to 6
- q_temporal: bfloat16 [256, 384, 576], P('sample', ('outer', 'inner')), parts along dimension 0, may hold values from -6 to 6
- k_temporal: bfloat16 [256, 384, 576], P('sample', ('outer', 'inner')), parts along dimension 0, may hold values from -6 to 6
- v_temporal: bfloat16 [256, 384, 576], P('sample', ('outer', 'inner')), parts along dimension 0, may hold values from -6 to 6
Outputs:
- middle_grad: bfloat16 [256, 384, 1152], P(('sample', 'outer', 'inner')), parts along dimension 0
- temporal_grads: bfloat16 [256, 384, 1728], P(('sample', 'outer', 'inner')), parts along dimension 0
The draws below stay inside these ranges and needn't reach their ends.
There are 2 independent parts, one for each index of `sample`. The reference program is written for one: setup_inputs(seed, part) draws one part's arguments, and reference() takes and returns one part's arrays. A program takes and returns all parts, laid end to end along the dimension named above; an argument that names none is the same for every part. Nothing has to cross between parts.
All inputs are finite; a program needn't handle non-finite values.
Results may differ from the reference program's by a relative error of at most 0.015.
Values may be sent and summed in bfloat16 or wider, within the bound.
A program may use at most 64 MiB of HBM per device.

```python
import jax
import jax.numpy as jnp
from jax import lax

D = 1152
HEADS = 8
HEAD_DIM = 72
S = 384
FRAMES = 128


def drawn(key, salt):
    channels = HEADS * HEAD_DIM
    salted = jax.random.fold_in(key, salt)
    query_all = jnp.clip(jax.random.normal(jax.random.fold_in(salted, 1), (FRAMES, S, channels), jnp.float32), -4.5, 4.5)
    key_all = jnp.clip(jax.random.normal(jax.random.fold_in(salted, 2), (FRAMES, S, channels), jnp.float32), -4.5, 4.5)
    return (query_all, key_all)


def draw_q_spatial(key, part):
    return drawn(key, 11)[0].astype(jnp.bfloat16)


def draw_k_spatial(key, part):
    return drawn(key, 11)[1].astype(jnp.bfloat16)


def draw_q_temporal(key, part):
    return drawn(key, 23)[0].astype(jnp.bfloat16)


def draw_k_temporal(key, part):
    return drawn(key, 23)[1].astype(jnp.bfloat16)


def steps_of(stream_key, dims, shards, smallest, largest):
    def one(dim, shards_of):
        steps = jax.random.uniform(jax.random.fold_in(jax.random.fold_in(stream_key, 6), dim), (shards_of,), jnp.float32, smallest / len(shards), largest / len(shards))
        return jnp.repeat(jnp.exp(steps), dims[dim] // shards_of).reshape((-1,) + (1,) * (len(dims) - dim - 1))

    gain = one(*shards[0])
    for cut in shards[1:]:
        gain = gain * one(*cut)
    return gain


def noise(key, extent, spread, limit, shards=(), kind=jnp.bfloat16):
    array = spread * jax.random.normal(key, extent, jnp.float32)
    if shards:
        array = array * steps_of(key, extent, shards, -0.22, 0.18)
    return jnp.clip(array, -limit, limit).astype(kind)


def setup_inputs(seed: int = 0, part: int = 0) -> dict:
    seeds = jax.random.split(jax.random.key(seed), 11)
    part_splits = jax.random.split(jax.random.fold_in(seeds[10], part), 11)
    out_cotangent = noise(part_splits[0], (FRAMES, S, D), 1.0, 6.0, ((0, 128),))
    wo_spatial = noise(seeds[1], (HEADS * HEAD_DIM, D), HEAD_DIM ** -0.5, 0.75)
    wqkv_spatial = noise(seeds[2], (D, 3 * HEADS * HEAD_DIM), D ** -0.5, 0.1875)
    wo_temporal = noise(seeds[3], (HEADS * HEAD_DIM, D), HEAD_DIM ** -0.5, 0.75)
    q_spatial = draw_q_spatial(jax.random.fold_in(jax.random.fold_in(seeds[10], part), 71), part)
    k_spatial = draw_k_spatial(jax.random.fold_in(jax.random.fold_in(seeds[10], part), 71), part)
    v_spatial = noise(part_splits[6], (FRAMES, S, HEADS * HEAD_DIM), 1.0, 6.0, ((0, 128),))
    q_temporal = draw_q_temporal(jax.random.fold_in(jax.random.fold_in(seeds[10], part), 71), part)
    k_temporal = draw_k_temporal(jax.random.fold_in(jax.random.fold_in(seeds[10], part), 71), part)
    v_temporal = noise(part_splits[9], (FRAMES, S, HEADS * HEAD_DIM), 1.0, 6.0, ((1, 128),))
    return {"out_cotangent": out_cotangent, "wo_spatial": wo_spatial, "wqkv_spatial": wqkv_spatial, "wo_temporal": wo_temporal, "q_spatial": q_spatial, "k_spatial": k_spatial, "v_spatial": v_spatial, "q_temporal": q_temporal, "k_temporal": k_temporal, "v_temporal": v_temporal}


def attend_back(queries, key_rows, value_rows, grad_out):
    scaling = queries.shape[-1] ** -0.5
    q_full = queries.astype(jnp.float32)
    k_full = key_rows.astype(jnp.float32)
    v_full = value_rows.astype(jnp.float32)
    g_full = grad_out.astype(jnp.float32)
    scores = jnp.einsum('lbhe,mbhe->bhlm', q_full, k_full) * scaling
    row_max = jnp.max(scores, axis=-1, keepdims=True)
    weights = jnp.exp(scores - row_max)
    weights = weights / jnp.sum(weights, axis=-1, keepdims=True)
    weights_low = lax.optimization_barrier(weights.astype(jnp.bfloat16)).astype(jnp.float32)
    grad_value = jnp.einsum('bhlm,lbhe->mbhe', weights_low, g_full).astype(jnp.bfloat16)
    grad_weight = jnp.einsum('lbhe,mbhe->bhlm', g_full, v_full)
    row_inner = jnp.sum(weights * grad_weight, axis=-1, keepdims=True)
    grad_score = lax.optimization_barrier((weights * (grad_weight - row_inner)).astype(jnp.bfloat16)).astype(jnp.float32)
    grad_query = (jnp.einsum('bhlm,mbhe->lbhe', grad_score, k_full) * scaling).astype(jnp.bfloat16)
    grad_key = (jnp.einsum('bhlm,lbhe->mbhe', grad_score, q_full) * scaling).astype(jnp.bfloat16)
    return grad_query, grad_key, grad_value


def block_grads(items):
    queries, key_rows, value_rows, grad_out = items
    length = queries.shape[0]
    channels = queries.shape[1]
    shaped = [a.reshape(length, 1, HEADS, HEAD_DIM) for a in (queries, key_rows, value_rows, grad_out)]
    grad_query, grad_key, grad_value = attend_back(shaped[0], shaped[1], shaped[2], shaped[3])
    return jnp.concatenate([grad_query.reshape(length, channels), grad_key.reshape(length, channels), grad_value.reshape(length, channels)], axis=1)


def reference(out_cotangent, wo_spatial, wqkv_spatial, wo_temporal, q_spatial, k_spatial, v_spatial, q_temporal, k_temporal, v_temporal):
    channels = HEADS * HEAD_DIM
    grad_rows = out_cotangent.reshape(FRAMES * S, D)
    spatial_out = jnp.dot(grad_rows, wo_spatial.T, preferred_element_type=jnp.float32).astype(jnp.bfloat16)
    spatial_out = spatial_out.reshape(FRAMES, S, channels)
    spatial_grads = lax.map(block_grads, (q_spatial, k_spatial, v_spatial, spatial_out))
    spatial_term = jnp.dot(spatial_grads.reshape(FRAMES * S, 3 * channels), wqkv_spatial.T, preferred_element_type=jnp.float32)
    middle = (grad_rows.astype(jnp.float32) + spatial_term).astype(jnp.bfloat16)
    temporal_out = jnp.dot(middle, wo_temporal.T, preferred_element_type=jnp.float32).astype(jnp.bfloat16)
    temporal_out = temporal_out.reshape(FRAMES, S, channels)
    swapped = tuple(jnp.swapaxes(a, 0, 1) for a in (q_temporal, k_temporal, v_temporal, temporal_out))
    temporal_grads = jnp.swapaxes(lax.map(block_grads, swapped), 0, 1)
    return middle.reshape(FRAMES, S, D), temporal_grads
```

```python
import functools

import jax
import jax.numpy as jnp
from jax import lax
from jax.experimental import pallas as pl
from jax.experimental.pallas import tpu as pltpu
from jax.sharding import PartitionSpec as P

HEADS = 8
HEAD = 72
PAIR = 2 * HEAD
CH = HEADS * HEAD
PAIRS = HEADS // 2
TOKENS = 384
FRAMES = 128
POS = 3
FEATURES = 1152
SLOTS1 = 7
SLOTS2 = 21
CHUNKS1 = ((0, 3), (3, 7))
CHUNKS2 = ((0, 3), (3, 9), (9, 15), (15, 21))
SCALE = HEAD ** -0.5
LOG2E = 1.4426950408889634
F32 = jnp.float32
BF16 = jnp.bfloat16


def dot(a, b, ca, cb):
    return lax.dot_general(a, b, (((ca,), (cb,)), ((), ())), preferred_element_type=F32)


def nn(a, b):
    return dot(a, b, 1, 0)


def nt(a, b):
    return dot(a, b, 1, 1)


def tn(a, b):
    return dot(a, b, 0, 0)


def coords():
    outer, inner = lax.axis_index("outer"), lax.axis_index("inner")
    y = outer * 2 + lax.div(inner, 32)
    z = lax.rem(lax.div(inner, 4), 8)
    x = lax.rem(inner, 4)
    return y, z, x


def device(y, z, x):
    return (lax.axis_index("sample"), lax.div(y, 2), lax.rem(y, 2) * 32 + z * 4 + x)


def peer(step):
    y, z, x = coords()
    shift = lax.rem(step * 5, 128)
    ty = lax.rem(y + lax.div(shift, 32), 4)
    tz = lax.rem(z + lax.rem(lax.div(shift, 4), 8), 8)
    tx = lax.rem(x + lax.rem(shift, 4), 4)
    return (ty * 8 + tz) * 4 + tx, device(ty, tz, tx)


def my_index():
    return lax.axis_index("outer") * 64 + lax.axis_index("inner")


def enter():
    barrier = pltpu.get_barrier_semaphore()

    def body(step, carry):
        _, dev = peer(step)
        pl.semaphore_signal(barrier, inc=1, device_id=dev, device_id_type=pl.DeviceIdType.MESH)
        return carry

    lax.fori_loop(1, FRAMES, body, 0)


def entered():
    pl.semaphore_wait(pltpu.get_barrier_semaphore(), FRAMES - 1)


def send(stage, recv, send_sem, recv_sem, lo, hi):
    mine = pl.ds(pl.multiple_of(my_index() * 2, 2), 2)
    land = recv.at[lo:hi, mine]
    pltpu.make_async_copy(stage.at[lo:hi, mine], land, recv_sem).start()

    def body(step, carry):
        index, dev = peer(step)
        pltpu.make_async_remote_copy(
            src_ref=stage.at[lo:hi, pl.ds(pl.multiple_of(index * 2, 2), 2)],
            dst_ref=land,
            send_sem=send_sem,
            recv_sem=recv_sem,
            device_id=dev,
            device_id_type=pl.DeviceIdType.MESH,
        ).start()
        return carry

    lax.fori_loop(1, FRAMES, body, 0)


def arrived(recv, sem, lo, hi):
    pltpu.make_async_copy(recv.at[lo:hi], recv.at[lo:hi], sem).wait()


def sent(stage, sem):
    part = stage.at[:, : 2 * (FRAMES - 1)]
    pltpu.make_async_copy(part, part, sem).wait()


def softmax_t(scores):
    top = jnp.max(scores, axis=0, keepdims=True)
    weights = jnp.exp2((scores - top) * (SCALE * LOG2E))
    return weights * (1.0 / jnp.sum(weights, axis=0, keepdims=True))


def grads_t(weights, weights_low, query, key, value, grad):
    grad_value = nt(grad, weights_low)
    grad_weight = tn(value, grad)
    inner = jnp.sum(weights * grad_weight, axis=0, keepdims=True)
    grad_score = (weights * (grad_weight - inner)).astype(BF16)
    grad_query = nn(key, grad_score) * SCALE
    grad_key = nt(query, grad_score) * SCALE
    return grad_query, grad_key, grad_value


def kernel(
    cot_h, wos_h, w_h, wot_h, qs_h, ks_h, vs_h, qt_h, kt_h, vt_h,
    mid_o, out_o,
    cot, wos, w, wot, qs, ks, vs, qt, kt, vt,
    gs, sgt, sg, pt, gt, rt, e01, e20, e21, weave,
    stage1, recv1, stage2, recv2,
    in_sem, send1, recv1_sem, send2, recv2_sem,
):
    loads = []
    order = ((cot_h, cot), (wos_h, wos), (qs_h, qs), (ks_h, ks), (vs_h, vs), (w_h, w), (wot_h, wot), (qt_h, qt), (kt_h, kt), (vt_h, vt))
    for i, (src, dst) in enumerate(order):
        copy = pltpu.make_async_copy(src, dst, in_sem.at[i])
        copy.start()
        loads.append(copy)
    enter()

    row = lax.broadcasted_iota(jnp.int32, (2 * FRAMES, TOKENS), 0)
    col = lax.broadcasted_iota(jnp.int32, (2 * FRAMES, TOKENS), 1)
    half, index = row & 1, row >> 1
    e01[...] = (col == 3 * index + half).astype(F32).astype(BF16)
    e20[...] = ((col == 3 * index + 2) & (half == 0)).astype(F32).astype(BF16)
    e21[...] = ((col == 3 * index + 2) & (half == 1)).astype(F32).astype(BF16)
    row = lax.broadcasted_iota(jnp.int32, (2 * FRAMES, 2 * FRAMES), 0)
    col = lax.broadcasted_iota(jnp.int32, (2 * FRAMES, 2 * FRAMES), 1)
    weave[...] = (col == (row & 1) * FRAMES + (row >> 1)).astype(F32).astype(BF16)

    loads[0].wait()
    loads[1].wait()
    gs[...] = nt(wos[...], cot[...]).astype(BF16)
    for i in (2, 3, 4):
        loads[i].wait()

    def spatial(p, carry):
        rows = pl.ds(pl.multiple_of(p * PAIR, 16), PAIR)
        q2, k2, v2, g2 = qs[rows], ks[rows], vs[rows], gs[rows]
        outs = []
        for i in range(2):
            cut = slice(i * HEAD, (i + 1) * HEAD)
            q, k, v, g = q2[cut], k2[cut], v2[cut], g2[cut]
            weights = softmax_t(tn(k, q))
            outs.append(grads_t(weights, weights.astype(BF16), q, k, v, g))
        for kind in range(3):
            both = jnp.concatenate([outs[0][kind], outs[1][kind]], axis=0).astype(BF16)
            sgt[pl.ds(pl.multiple_of(kind * CH + p * PAIR, 16), PAIR)] = both
        return carry

    lax.fori_loop(0, PAIRS, spatial, 0)
    sg[...] = sgt[...].T
    loads[5].wait()

    def project(n, carry):
        cols = pl.ds(pl.multiple_of(n * 384, 128), 384)
        mid_o[:, cols] = (cot[:, cols].astype(F32) + nn(sg[...], w[:, cols])).astype(BF16)
        return carry

    lax.fori_loop(0, FEATURES // 384, project, 0)
    loads[6].wait()
    entered()

    low = nt(mid_o[...], wot[0:256]).astype(BF16)
    stage1[0] = nn(e01[...], low[:, 0:128]).astype(BF16)
    stage1[1] = nn(e01[...], low[:, 128:256]).astype(BF16)
    stage1[2] = (nn(e20[...], low[:, 0:128]) + nn(e21[...], low[:, 128:256])).astype(BF16)
    send(stage1, recv1, send1, recv1_sem.at[0], *CHUNKS1[0])
    high = nt(mid_o[...], wot[256:576]).astype(BF16)
    stage1[3] = nn(e01[...], high[:, 0:128]).astype(BF16)
    stage1[4] = nn(e01[...], high[:, 128:256]).astype(BF16)
    stage1[5] = (nn(e20[...], high[:, 0:128]) + nn(e21[...], high[:, 128:256])).astype(BF16)
    rest = high[:, 256:320]
    stage1[6] = jnp.concatenate([nn(e01[...], rest), nn(e20[...], rest)], axis=1).astype(BF16)
    send(stage1, recv1, send1, recv1_sem.at[1], *CHUNKS1[1])

    for i in (7, 8, 9):
        loads[i].wait()

    def prepare(i, carry):
        j, p = lax.div(i, PAIRS), lax.rem(i, PAIRS)
        rows = pl.ds(pl.multiple_of(p * PAIR, 16), PAIR)
        q2, k2 = qt[j, rows], kt[j, rows]
        for h in range(2):
            cut = slice(h * HEAD, (h + 1) * HEAD)
            pt[j, p, h] = softmax_t(tn(k2[cut], q2[cut]))
        return carry

    lax.fori_loop(0, POS * PAIRS, prepare, 0)

    def unpack1(base, c):
        for i in range(2):
            block = tn(recv1[base + i], weave[...]).astype(BF16)
            rows = slice((c + i) * 128, (c + i + 1) * 128)
            gt[0, rows] = block[:, :128]
            gt[1, rows] = block[:, 128:]
        block = tn(recv1[base + 2], weave[...]).astype(BF16)
        gt[2, c * 128 : (c + 1) * 128] = block[:, :128]
        gt[2, (c + 1) * 128 : (c + 2) * 128] = block[:, 128:]

    def temporal(p):
        def body(j, carry):
            rows = slice(p * PAIR, (p + 1) * PAIR)
            q2, k2, v2, g2 = qt[j, rows], kt[j, rows], vt[j, rows], gt[j, rows]
            outs = []
            for h in range(2):
                cut = slice(h * HEAD, (h + 1) * HEAD)
                weights = pt[j, p, h]
                outs.append(grads_t(weights, weights.astype(BF16), q2[cut], k2[cut], v2[cut], g2[cut]))
            for kind in range(3):
                both = jnp.concatenate([outs[0][kind], outs[1][kind]], axis=0).astype(BF16)
                rt[j, (p * 3 + kind) * PAIR : (p * 3 + kind + 1) * PAIR] = both
            return carry

        lax.fori_loop(0, POS, body, 0)

    def pack2(t, c):
        wide = min(128, 3 * CH - (c + 1) * 128)
        for i, width in ((0, 128), (1, wide)):
            rows = slice((c + i) * 128, (c + i) * 128 + width)
            both = jnp.concatenate([rt[0, rows], rt[1, rows]], axis=1)
            stage2[t + i, :, 0:width] = nt(weave[...], both).astype(BF16)
        first = nt(weave[:, :128], rt[2, c * 128 : (c + 1) * 128])
        second = nt(weave[:, 128:], rt[2, (c + 1) * 128 : (c + 1) * 128 + wide])
        if wide < 128:
            second = jnp.concatenate([second, jnp.zeros((2 * FRAMES, 128 - wide), F32)], axis=1)
        stage2[t + 2] = (first + second).astype(BF16)

    arrived(recv1, recv1_sem.at[0], *CHUNKS1[0])
    unpack1(0, 0)
    temporal(0)
    pack2(0, 0)
    send(stage2, recv2, send2, recv2_sem.at[0], *CHUNKS2[0])

    arrived(recv1, recv1_sem.at[1], *CHUNKS1[1])
    unpack1(3, 2)
    block = tn(recv1[6], weave[...]).astype(BF16)
    gt[0, 512:576] = block[:64, :128]
    gt[1, 512:576] = block[:64, 128:]
    gt[2, 512:576] = block[64:, :128]
    for p in range(1, PAIRS):
        temporal(p)
        lo, hi = CHUNKS2[p]
        for t in range(lo, hi, 3):
            pack2(t, t // 3 * 2)
        send(stage2, recv2, send2, recv2_sem.at[p], lo, hi)

    def put(c, block):
        start, width = c * 128, block.shape[0]
        at = start
        while at < start + width:
            unit = at // PAIR
            stop = min((unit + 1) * PAIR, start + width)
            p, kind = unit // 3, unit % 3
            dest = kind * CH + p * PAIR + at - unit * PAIR
            out_o[dest : dest + stop - at] = block[at - start : stop - start]
            at = stop

    def unpack2(t, c):
        wide = min(128, 3 * CH - (c + 1) * 128)
        pair = recv2[t + 2]
        put(c, (tn(recv2[t], e01[...]) + tn(pair, e20[...])).astype(BF16))
        last = (tn(recv2[t + 1], e01[...]) + tn(pair, e21[...])).astype(BF16)
        put(c + 1, last[:wide])

    for p in range(PAIRS):
        lo, hi = CHUNKS2[p]
        arrived(recv2, recv2_sem.at[p], lo, hi)
        for t in range(lo, hi, 3):
            unpack2(t, t // 3 * 2)
    sent(stage1, send1)
    sent(stage2, send2)


def local(cot, wos, wqkv, wot, qs, ks, vs, qt, kt, vt):
    def flip(a):
        return a[0].T

    def turn(a):
        return jnp.transpose(a, (1, 2, 0))

    vmem = pl.BlockSpec(memory_space=pltpu.VMEM)
    hbm = pl.BlockSpec(memory_space=pl.ANY)
    spatial = pltpu.VMEM((CH, TOKENS), BF16)
    temporal = pltpu.VMEM((POS, CH, FRAMES), BF16)
    pick = pltpu.VMEM((2 * FRAMES, TOKENS), BF16)
    middle, grads = pl.pallas_call(
        kernel,
        out_shape=(
            jax.ShapeDtypeStruct((TOKENS, FEATURES), BF16),
            jax.ShapeDtypeStruct((3 * CH, TOKENS), BF16),
        ),
        in_specs=[hbm] * 10,
        out_specs=(vmem, vmem),
        scratch_shapes=[
            pltpu.VMEM((TOKENS, FEATURES), BF16),
            pltpu.VMEM((CH, FEATURES), BF16),
            pltpu.VMEM((3 * CH, FEATURES), BF16),
            pltpu.VMEM((CH, FEATURES), BF16),
            spatial, spatial, spatial,
            temporal, temporal, temporal,
            spatial,
            pltpu.VMEM((3 * CH, TOKENS), BF16),
            pltpu.VMEM((TOKENS, 3 * CH), BF16),
            pltpu.VMEM((POS, PAIRS, 2, FRAMES, FRAMES), F32),
            temporal,
            pltpu.VMEM((POS, 3 * CH, FRAMES), BF16),
            pick, pick, pick,
            pltpu.VMEM((2 * FRAMES, 2 * FRAMES), BF16),
            pltpu.VMEM((SLOTS1, 2 * FRAMES, 128), BF16),
            pltpu.VMEM((SLOTS1, 2 * FRAMES, 128), BF16),
            pltpu.VMEM((SLOTS2, 2 * FRAMES, 128), BF16),
            pltpu.VMEM((SLOTS2, 2 * FRAMES, 128), BF16),
            pltpu.SemaphoreType.DMA((10,)),
            pltpu.SemaphoreType.DMA,
            pltpu.SemaphoreType.DMA((len(CHUNKS1),)),
            pltpu.SemaphoreType.DMA,
            pltpu.SemaphoreType.DMA((len(CHUNKS2),)),
        ],
        compiler_params=pltpu.CompilerParams(
            collective_id=0, has_side_effects=True, vmem_limit_bytes=56 << 20
        ),
        name="reward_backward",
    )(
        cot[0], wos, wqkv.T, wot,
        flip(qs), flip(ks), flip(vs),
        turn(qt), turn(kt), turn(vt),
    )
    return middle[None], grads.T[None]


def solution(mesh):
    frames = P(("sample", "outer", "inner"), None, None)
    positions = P("sample", ("outer", "inner"), None)
    return jax.shard_map(
        local,
        mesh=mesh,
        in_specs=(frames, P(), P(), P(), frames, frames, frames, positions, positions, positions),
        out_specs=(frames, frames),
        check_vma=False,
    )
```

```python
import functools

import jax
import jax.numpy as jnp
from jax import lax
from jax.experimental import pallas as pl
from jax.experimental.pallas import tpu as pltpu
from jax.sharding import PartitionSpec as P

HEADS = 8
HEAD = 72
PAIR = 2 * HEAD
CH = HEADS * HEAD
PAIRS = HEADS // 2
TOKENS = 384
FRAMES = 128
POS = 3
FEATURES = 1152
SLOTS1 = 7
SLOTS2 = 21
CHUNKS1 = ((0, 3), (3, 7))
CHUNKS2 = ((0, 3), (3, 9), (9, 15), (15, 21))
SCALE = HEAD ** -0.5
LOG2E = 1.4426950408889634
F32 = jnp.float32
BF16 = jnp.bfloat16


def dot(a, b, ca, cb):
    return lax.dot_general(a, b, (((ca,), (cb,)), ((), ())), preferred_element_type=F32)


def nn(a, b):
    return dot(a, b, 1, 0)


def nt(a, b):
    return dot(a, b, 1, 1)


def tn(a, b):
    return dot(a, b, 0, 0)


def coords():
    outer, inner = lax.axis_index("outer"), lax.axis_index("inner")
    y = outer * 2 + lax.div(inner, 32)
    z = lax.rem(lax.div(inner, 4), 8)
    x = lax.rem(inner, 4)
    return y, z, x


def device(y, z, x):
    return lax.axis_index("sample") * FRAMES + (y * 8 + z) * 4 + x


def my_index():
    return lax.axis_index("outer") * 64 + lax.axis_index("inner")


def greet(sem, line):
    y, z, x = coords()
    if line == "x":
        peers = [(y, z, lax.rem(x + i, 4)) for i in range(1, 4)]
    elif line == "y":
        peers = [(lax.rem(y + i, 4), z, x) for i in range(1, 4)]
    else:
        peers = [(y, lax.rem(z + i, 8), x) for i in range(1, 8)]
    for peer in peers:
        pl.semaphore_signal(
            sem, inc=1, device_id=device(*peer), device_id_type=pl.DeviceIdType.LOGICAL
        )


def enter():
    barrier = pltpu.get_barrier_semaphore()
    for line in "zyx":
        greet(barrier, line)


def lines_entered(sem):
    pl.semaphore_wait(pltpu.get_barrier_semaphore(), 13)
    greet(sem, "x")


def planes_entered(sems):
    pl.semaphore_wait(sems.at[0], 3)
    greet(sems.at[1], "y")


def entered(sem):
    pl.semaphore_wait(sem, 3)


def send(stage, recv, send_sem, recv_sem, lo, hi):
    me = my_index()
    sample = lax.axis_index("sample")
    y, z, x = coords()
    sign = 1 - 2 * sample
    depth = [lax.rem(z + sign * i + 8, 8) * 4 for i in range(8)]
    land = recv.at[lo:hi, pl.ds(pl.multiple_of(me * 2, 2), 2)]
    pltpu.make_async_copy(stage.at[lo:hi, pl.ds(pl.multiple_of(me * 2, 2), 2)], land, recv_sem).start()

    def one(across, away):
        ty = lax.rem(y + sign * lax.div(across, 4) + 4, 4)
        tx = lax.rem(x + sign * lax.rem(across, 4) + 4, 4)
        index = ty * 32 + depth[away] + tx
        pltpu.make_async_remote_copy(
            src_ref=stage.at[lo:hi, pl.ds(pl.multiple_of(index * 2, 2), 2)],
            dst_ref=land,
            send_sem=send_sem,
            recv_sem=recv_sem,
            device_id=sample * FRAMES + index,
            device_id_type=pl.DeviceIdType.LOGICAL,
        ).start()

    def body(turn, carry):
        for i, away in enumerate((4, 1, 7, 2, 6, 3, 5)):
            one(lax.rem(turn + 5 * i + 5, 16), away)
        one(turn + 1, 0)
        return carry

    lax.fori_loop(0, 15, body, 0)
    for i, away in enumerate((4, 1, 7, 2, 6, 3, 5)):
        one((15 + 5 * i + 5) % 16, away)


def arrived(recv, sem, lo, hi):
    pltpu.make_async_copy(recv.at[lo:hi], recv.at[lo:hi], sem).wait()


def sent(stage, sem):
    part = stage.at[:, : 2 * (FRAMES - 1)]
    pltpu.make_async_copy(part, part, sem).wait()


def softmax_t(scores):
    top = jnp.max(scores, axis=0, keepdims=True)
    weights = jnp.exp2((scores - top) * (SCALE * LOG2E))
    return weights * (1.0 / jnp.sum(weights, axis=0, keepdims=True))


def grads_t(weights, weights_low, query, key, value, grad):
    grad_value = nt(grad, weights_low)
    grad_weight = tn(value, grad)
    inner = jnp.sum(weights * grad_weight, axis=0, keepdims=True)
    grad_score = (weights * (grad_weight - inner)).astype(BF16)
    grad_query = nn(key, grad_score) * SCALE
    grad_key = nt(query, grad_score) * SCALE
    return grad_query, grad_key, grad_value


def picks(e01, e20, e21):
    row = lax.broadcasted_iota(jnp.int32, (2 * FRAMES, TOKENS), 0)
    col = lax.broadcasted_iota(jnp.int32, (2 * FRAMES, TOKENS), 1)
    half, index = row & 1, row >> 1
    e01[...] = (col == 3 * index + half).astype(F32).astype(BF16)
    e20[...] = ((col == 3 * index + 2) & (half == 0)).astype(F32).astype(BF16)
    e21[...] = ((col == 3 * index + 2) & (half == 1)).astype(F32).astype(BF16)


def kernel(
    cot_h, wos_h, w_h, wot_h, qs_h, ks_h, vs_h, qt_h, kt_h, vt_h,
    mid_o, recv2,
    cot, wos, w, wot, qs, ks, vs, qt, kt, vt,
    mid, gs, sgt, sg, pt, gt, rt, e01, e20, e21, weave,
    stage1, recv1, stage2,
    in_sem, mid_sem, send1, recv1_sem, send2, recv2_sem, line_sem,
):
    loads = []
    order = ((cot_h, cot), (wos_h, wos), (qs_h, qs), (ks_h, ks), (vs_h, vs), (w_h, w), (wot_h, wot), (qt_h, qt), (kt_h, kt), (vt_h, vt))
    for i, (src, dst) in enumerate(order):
        copy = pltpu.make_async_copy(src, dst, in_sem.at[i])
        copy.start()
        loads.append(copy)
    enter()

    picks(e01, e20, e21)
    row = lax.broadcasted_iota(jnp.int32, (2 * FRAMES, 2 * FRAMES), 0)
    col = lax.broadcasted_iota(jnp.int32, (2 * FRAMES, 2 * FRAMES), 1)
    weave[...] = (col == (row & 1) * FRAMES + (row >> 1)).astype(F32).astype(BF16)

    loads[0].wait()
    loads[1].wait()
    gs[...] = nt(wos[...], cot[...]).astype(BF16)
    lines_entered(line_sem.at[0])
    for i in (2, 3, 4):
        loads[i].wait()

    def spatial(p, carry):
        rows = pl.ds(pl.multiple_of(p * PAIR, 16), PAIR)
        q2, k2, v2, g2 = qs[rows], ks[rows], vs[rows], gs[rows]
        outs = []
        for i in range(2):
            cut = slice(i * HEAD, (i + 1) * HEAD)
            q, k, v, g = q2[cut], k2[cut], v2[cut], g2[cut]
            weights = softmax_t(tn(k, q))
            outs.append(grads_t(weights, weights.astype(BF16), q, k, v, g))
        for kind in range(3):
            both = jnp.concatenate([outs[0][kind], outs[1][kind]], axis=0).astype(BF16)
            sgt[pl.ds(pl.multiple_of(kind * CH + p * PAIR, 16), PAIR)] = both
        return carry

    lax.fori_loop(0, PAIRS, spatial, 0)
    planes_entered(line_sem)
    sg[...] = sgt[...].T
    loads[5].wait()

    def project(n, carry):
        cols = pl.ds(pl.multiple_of(n * 384, 128), 384)
        mid[:, cols] = (cot[:, cols].astype(F32) + nn(sg[...], w[:, cols])).astype(BF16)
        return carry

    lax.fori_loop(0, FEATURES // 384, project, 0)
    keep = pltpu.make_async_copy(mid, mid_o, mid_sem)
    keep.start()
    loads[6].wait()
    entered(line_sem.at[1])

    low = nt(mid[...], wot[0:256]).astype(BF16)
    stage1[0] = nn(e01[...], low[:, 0:128]).astype(BF16)
    stage1[1] = nn(e01[...], low[:, 128:256]).astype(BF16)
    stage1[2] = (nn(e20[...], low[:, 0:128]) + nn(e21[...], low[:, 128:256])).astype(BF16)
    send(stage1, recv1, send1, recv1_sem.at[0], *CHUNKS1[0])
    high = nt(mid[...], wot[256:576]).astype(BF16)
    stage1[3] = nn(e01[...], high[:, 0:128]).astype(BF16)
    stage1[4] = nn(e01[...], high[:, 128:256]).astype(BF16)
    stage1[5] = (nn(e20[...], high[:, 0:128]) + nn(e21[...], high[:, 128:256])).astype(BF16)
    rest = high[:, 256:320]
    stage1[6] = jnp.concatenate([nn(e01[...], rest), nn(e20[...], rest)], axis=1).astype(BF16)
    send(stage1, recv1, send1, recv1_sem.at[1], *CHUNKS1[1])

    for i in (7, 8, 9):
        loads[i].wait()

    def prepare(i, carry):
        j, p = lax.div(i, PAIRS), lax.rem(i, PAIRS)
        rows = pl.ds(pl.multiple_of(p * PAIR, 16), PAIR)
        q2, k2 = qt[j, rows], kt[j, rows]
        for h in range(2):
            cut = slice(h * HEAD, (h + 1) * HEAD)
            pt[j, p, h] = softmax_t(tn(k2[cut], q2[cut]))
        return carry

    lax.fori_loop(0, POS * PAIRS, prepare, 0)

    def unpack1(base, c):
        for i in range(2):
            block = tn(recv1[base + i], weave[...]).astype(BF16)
            rows = slice((c + i) * 128, (c + i + 1) * 128)
            gt[0, rows] = block[:, :128]
            gt[1, rows] = block[:, 128:]
        block = tn(recv1[base + 2], weave[...]).astype(BF16)
        gt[2, c * 128 : (c + 1) * 128] = block[:, :128]
        gt[2, (c + 1) * 128 : (c + 2) * 128] = block[:, 128:]

    def temporal(p):
        def body(j, carry):
            rows = slice(p * PAIR, (p + 1) * PAIR)
            q2, k2, v2, g2 = qt[j, rows], kt[j, rows], vt[j, rows], gt[j, rows]
            outs = []
            for h in range(2):
                cut = slice(h * HEAD, (h + 1) * HEAD)
                weights = pt[j, p, h]
                outs.append(grads_t(weights, weights.astype(BF16), q2[cut], k2[cut], v2[cut], g2[cut]))
            for kind in range(3):
                both = jnp.concatenate([outs[0][kind], outs[1][kind]], axis=0).astype(BF16)
                rt[j, (p * 3 + kind) * PAIR : (p * 3 + kind + 1) * PAIR] = both
            return carry

        lax.fori_loop(0, POS, body, 0)

    def pack2(t, c):
        wide = min(128, 3 * CH - (c + 1) * 128)
        for i, width in ((0, 128), (1, wide)):
            rows = slice((c + i) * 128, (c + i) * 128 + width)
            both = jnp.concatenate([rt[0, rows], rt[1, rows]], axis=1)
            stage2[t + i, :, 0:width] = nt(weave[...], both).astype(BF16)
        first = nt(weave[:, :128], rt[2, c * 128 : (c + 1) * 128])
        second = nt(weave[:, 128:], rt[2, (c + 1) * 128 : (c + 1) * 128 + wide])
        if wide < 128:
            second = jnp.concatenate([second, jnp.zeros((2 * FRAMES, 128 - wide), F32)], axis=1)
        stage2[t + 2] = (first + second).astype(BF16)

    arrived(recv1, recv1_sem.at[0], *CHUNKS1[0])
    unpack1(0, 0)
    temporal(0)
    pack2(0, 0)
    send(stage2, recv2, send2, recv2_sem.at[0], *CHUNKS2[0])

    arrived(recv1, recv1_sem.at[1], *CHUNKS1[1])
    unpack1(3, 2)
    block = tn(recv1[6], weave[...]).astype(BF16)
    gt[0, 512:576] = block[:64, :128]
    gt[1, 512:576] = block[:64, 128:]
    gt[2, 512:576] = block[64:, :128]
    for p in range(1, PAIRS):
        temporal(p)
        lo, hi = CHUNKS2[p]
        for t in range(lo, hi, 3):
            pack2(t, t // 3 * 2)
        send(stage2, recv2, send2, recv2_sem.at[p], lo, hi)

    for p in range(PAIRS):
        arrived(recv2, recv2_sem.at[p], *CHUNKS2[p])
    keep.wait()
    sent(stage1, send1)
    sent(stage2, send2)


def finish(mid_h, recv_h, mid_o, out_o, recv, out, mid, e01, e20, e21, in_sem, mid_sem, out_sem):
    fetch = pltpu.make_async_copy(mid_h, mid, mid_sem.at[0])
    keep = pltpu.make_async_copy(mid, mid_o, mid_sem.at[1])
    loads = [
        pltpu.make_async_copy(recv_h.at[t : t + 3], recv.at[t : t + 3], in_sem.at[t // 3])
        for t in range(0, SLOTS2, 3)
    ]
    for load in loads:
        load.start()
    fetch.start()
    picks(e01, e20, e21)

    def put(c, block):
        start, width = c * 128, block.shape[0]
        at = start
        while at < start + width:
            unit = at // PAIR
            stop = min((unit + 1) * PAIR, start + width)
            p, kind = unit // 3, unit % 3
            dest = kind * CH + p * PAIR + at - unit * PAIR
            out[dest : dest + stop - at] = block[at - start : stop - start]
            at = stop

    stores = []
    for t in range(0, SLOTS2, 3):
        loads[t // 3].wait()
        if t == 6:
            fetch.wait()
            keep.start()
        c = t // 3 * 2
        wide = min(128, 3 * CH - (c + 1) * 128)
        pair = recv[t + 2]
        put(c, (tn(recv[t], e01[...]) + tn(pair, e20[...])).astype(BF16))
        last = (tn(recv[t + 1], e01[...]) + tn(pair, e21[...])).astype(BF16)
        put(c + 1, last[:wide])
        for p in range(PAIRS):
            if c * 128 < 3 * PAIR * (p + 1) <= (c + 2) * 128:
                for kind in range(3):
                    rows = pl.ds(kind * CH + p * PAIR, PAIR)
                    copy = pltpu.make_async_copy(out.at[rows], out_o.at[rows], out_sem.at[p * 3 + kind])
                    copy.start()
                    stores.append(copy)
    keep.wait()
    for copy in stores:
        copy.wait()


def local(cot, wos, wqkv, wot, qs, ks, vs, qt, kt, vt):
    def flip(a):
        return a[0].T

    def turn(a):
        return jnp.transpose(a, (1, 2, 0))

    hbm = pl.BlockSpec(memory_space=pl.ANY)
    spatial = pltpu.VMEM((CH, TOKENS), BF16)
    temporal = pltpu.VMEM((POS, CH, FRAMES), BF16)
    pick = pltpu.VMEM((2 * FRAMES, TOKENS), BF16)
    middle, blocks = pl.pallas_call(
        kernel,
        out_shape=(
            jax.ShapeDtypeStruct((TOKENS, FEATURES), BF16),
            jax.ShapeDtypeStruct((SLOTS2, 2 * FRAMES, 128), BF16),
        ),
        in_specs=[hbm] * 10,
        out_specs=(hbm, hbm),
        scratch_shapes=[
            pltpu.VMEM((TOKENS, FEATURES), BF16),
            pltpu.VMEM((CH, FEATURES), BF16),
            pltpu.VMEM((3 * CH, FEATURES), BF16),
            pltpu.VMEM((CH, FEATURES), BF16),
            spatial, spatial, spatial,
            temporal, temporal, temporal,
            pltpu.VMEM((TOKENS, FEATURES), BF16),
            spatial,
            pltpu.VMEM((3 * CH, TOKENS), BF16),
            pltpu.VMEM((TOKENS, 3 * CH), BF16),
            pltpu.VMEM((POS, PAIRS, 2, FRAMES, FRAMES), F32),
            temporal,
            pltpu.VMEM((POS, 3 * CH, FRAMES), BF16),
            pick, pick, pick,
            pltpu.VMEM((2 * FRAMES, 2 * FRAMES), BF16),
            pltpu.VMEM((SLOTS1, 2 * FRAMES, 128), BF16),
            pltpu.VMEM((SLOTS1, 2 * FRAMES, 128), BF16),
            pltpu.VMEM((SLOTS2, 2 * FRAMES, 128), BF16),
            pltpu.SemaphoreType.DMA((10,)),
            pltpu.SemaphoreType.DMA,
            pltpu.SemaphoreType.DMA,
            pltpu.SemaphoreType.DMA((len(CHUNKS1),)),
            pltpu.SemaphoreType.DMA,
            pltpu.SemaphoreType.DMA((len(CHUNKS2),)),
            pltpu.SemaphoreType.REGULAR((2,)),
        ],
        compiler_params=pltpu.CompilerParams(
            collective_id=0, has_side_effects=True, vmem_limit_bytes=56 << 20
        ),
        name="reward_backward",
    )(
        cot[0], wos, wqkv.T, wot,
        flip(qs), flip(ks), flip(vs),
        turn(qt), turn(kt), turn(vt),
    )
    middle, grads = pl.pallas_call(
        finish,
        out_shape=(
            jax.ShapeDtypeStruct((TOKENS, FEATURES), BF16),
            jax.ShapeDtypeStruct((3 * CH, TOKENS), BF16),
        ),
        in_specs=[hbm] * 2,
        out_specs=(hbm, hbm),
        scratch_shapes=[
            pltpu.VMEM((SLOTS2, 2 * FRAMES, 128), BF16),
            pltpu.VMEM((3 * CH, TOKENS), BF16),
            pltpu.VMEM((TOKENS, FEATURES), BF16),
            pick, pick, pick,
            pltpu.SemaphoreType.DMA((SLOTS2 // 3,)),
            pltpu.SemaphoreType.DMA((2,)),
            pltpu.SemaphoreType.DMA((3 * PAIRS,)),
        ],
        compiler_params=pltpu.CompilerParams(vmem_limit_bytes=56 << 20),
        name="unpack",
    )(middle, blocks)
    return middle[None], grads.T[None]


def solution(mesh):
    frames = P(("sample", "outer", "inner"), None, None)
    positions = P("sample", ("outer", "inner"), None)
    return jax.shard_map(
        local,
        mesh=mesh,
        in_specs=(frames, P(), P(), P(), frames, frames, frames, positions, positions, positions),
        out_specs=(frames, frames),
        check_vma=False,
    )
```

```python
import functools

import jax
import jax.numpy as jnp
from jax import lax
from jax.experimental import pallas as pl
from jax.experimental.pallas import tpu as pltpu
from jax.sharding import PartitionSpec as P

HEADS = 8
HEAD = 72
CH = HEADS * HEAD
GROUPS = ((0, 3), (3, 6), (6, 8))
TOKENS = 384
FRAMES = 128
POS = 3
FEATURES = 1152
SLOTS = 4
AHEAD = 3
SLOTS1 = 7
SLOTS2 = 21
CHUNKS1 = ((0, 3), (3, 7))
CHUNKS2 = ((0, 6), (6, 15), (15, 21))
LAST = CHUNKS2[-1][0]
SPLIT = (432, 432, 416)
SCALE = HEAD ** -0.5
LOG2E = 1.4426950408889634
F32 = jnp.float32
BF16 = jnp.bfloat16


def dot(a, b, ca, cb):
    return lax.dot_general(a, b, (((ca,), (cb,)), ((), ())), preferred_element_type=F32)


def nn(a, b):
    return dot(a, b, 1, 0)


def nt(a, b):
    return dot(a, b, 1, 1)


def tn(a, b):
    return dot(a, b, 0, 0)


def coords():
    outer, inner = lax.axis_index("outer"), lax.axis_index("inner")
    y = outer * 2 + lax.div(inner, 32)
    z = lax.rem(lax.div(inner, 4), 8)
    x = lax.rem(inner, 4)
    return y, z, x


def device(y, z, x):
    return lax.axis_index("sample") * FRAMES + (y * 8 + z) * 4 + x


def my_index():
    return lax.axis_index("outer") * 64 + lax.axis_index("inner")


def greet(sem, line):
    y, z, x = coords()
    if line == "x":
        peers = [(y, z, lax.rem(x + i, 4)) for i in range(1, 4)]
    elif line == "y":
        peers = [(lax.rem(y + i, 4), z, x) for i in range(1, 4)]
    else:
        peers = [(y, lax.rem(z + i, 8), x) for i in range(1, 8)]
    for peer in peers:
        pl.semaphore_signal(
            sem, inc=1, device_id=device(*peer), device_id_type=pl.DeviceIdType.LOGICAL
        )


def enter():
    barrier = pltpu.get_barrier_semaphore()
    for line in "zyx":
        greet(barrier, line)


def lines_entered(sem):
    pl.semaphore_wait(pltpu.get_barrier_semaphore(), 13)
    greet(sem, "x")


def planes_entered(sems):
    pl.semaphore_wait(sems.at[0], 3)
    greet(sems.at[1], "y")


def entered(sem):
    pl.semaphore_wait(sem, 3)


def send(stage, recv, send_sem, recv_sem, lo, hi):
    me = my_index()
    sample = lax.axis_index("sample")
    y, z, x = coords()
    sign = 1 - 2 * sample
    depth = [lax.rem(z + sign * i + 8, 8) * 4 for i in range(8)]
    land = recv.at[lo:hi, pl.ds(pl.multiple_of(me * 2, 2), 2)]
    pltpu.make_async_copy(stage.at[lo:hi, pl.ds(pl.multiple_of(me * 2, 2), 2)], land, recv_sem).start()

    def one(across, away):
        ty = lax.rem(y + sign * lax.div(across, 4) + 4, 4)
        tx = lax.rem(x + sign * lax.rem(across, 4) + 4, 4)
        index = ty * 32 + depth[away] + tx
        pltpu.make_async_remote_copy(
            src_ref=stage.at[lo:hi, pl.ds(pl.multiple_of(index * 2, 2), 2)],
            dst_ref=land,
            send_sem=send_sem,
            recv_sem=recv_sem,
            device_id=sample * FRAMES + index,
            device_id_type=pl.DeviceIdType.LOGICAL,
        ).start()

    def body(turn, carry):
        for i, away in enumerate((4, 1, 7, 2, 6, 3, 5)):
            one(lax.rem(turn + 5 * i + 5, 16), away)
        one(turn + 1, 0)
        return carry

    lax.fori_loop(0, 15, body, 0)
    for i, away in enumerate((4, 1, 7, 2, 6, 3, 5)):
        one((15 + 5 * i + 5) % 16, away)


def arrived(recv, sem, lo, hi):
    pltpu.make_async_copy(recv.at[lo:hi], recv.at[lo:hi], sem).wait()


def sent(stage, sem):
    part = stage.at[:, : 2 * (FRAMES - 1)]
    pltpu.make_async_copy(part, part, sem).wait()


def softmax_t(scores):
    top = jnp.max(scores, axis=0, keepdims=True)
    weights = jnp.exp2((scores - top) * (SCALE * LOG2E))
    return weights * (1.0 / jnp.sum(weights, axis=0, keepdims=True))


def score_grad(weights, grad_weight):
    inner = jnp.sum(weights * grad_weight, axis=0, keepdims=True)
    return (weights * (grad_weight - inner)).astype(BF16)


def unpack2(recv, e01, e20, e21, out, lo, hi):
    def put(c, block):
        at, stop = c * 128, c * 128 + block.shape[0]
        for first, last in GROUPS:
            size = (last - first) * HEAD
            for kind in range(3):
                start = 3 * first * HEAD + kind * size
                a, b = max(at, start), min(stop, start + size)
                if a < b:
                    dest = kind * CH + first * HEAD + a - start
                    out[dest : dest + b - a] = block[a - at : b - at]

    for t in range(lo, hi, 3):
        c = t // 3 * 2
        wide = min(128, 3 * CH - (c + 1) * 128)
        pair = recv[t + 2]
        put(c, (tn(recv[t], e01[...]) + tn(pair, e20[...])).astype(BF16))
        last = (tn(recv[t + 1], e01[...]) + tn(pair, e21[...])).astype(BF16)
        put(c + 1, last[:wide])


def picks(e01, e20, e21):
    row = lax.broadcasted_iota(jnp.int32, (2 * FRAMES, TOKENS), 0)
    col = lax.broadcasted_iota(jnp.int32, (2 * FRAMES, TOKENS), 1)
    half, index = row & 1, row >> 1
    e01[...] = (col == 3 * index + half).astype(F32).astype(BF16)
    e20[...] = ((col == 3 * index + 2) & (half == 0)).astype(F32).astype(BF16)
    e21[...] = ((col == 3 * index + 2) & (half == 1)).astype(F32).astype(BF16)


def kernel(
    cot_h, wos_h, w_h, wot_h, qs_h, ks_h, vs_h, qt_h, kt_h, vt_h,
    mid, recv2, picked, part,
    cot, wos, w, wot, qs, ks, vs, qt, kt, vt,
    gs, sgt, sg, pt, gt, rt, weave,
    score, grad_weight, weight_low, grad_score, stage1, recv1, stage2,
    in_sem, send1, recv1_sem, send2, recv2_sem, line_sem,
):
    loads = []
    order = ((qs_h, qs), (ks_h, ks), (cot_h, cot), (wos_h, wos), (vs_h, vs), (w_h, w), (wot_h, wot), (qt_h, qt), (kt_h, kt), (vt_h, vt))
    for i, (src, dst) in enumerate(order):
        loads.append(pltpu.make_async_copy(src, dst, in_sem.at[i]))
    for copy in loads[:5]:
        copy.start()
    enter()

    e01, e20, e21 = (picked.at[i] for i in range(3))
    picks(e01, e20, e21)
    row = lax.broadcasted_iota(jnp.int32, (2 * FRAMES, 2 * FRAMES), 0)
    col = lax.broadcasted_iota(jnp.int32, (2 * FRAMES, 2 * FRAMES), 1)
    weave[...] = (col == (row & 1) * FRAMES + (row >> 1)).astype(F32).astype(BF16)

    def scores(h):
        rows = slice(h * HEAD, (h + 1) * HEAD)
        score[h % SLOTS] = tn(ks[rows], qs[rows])

    def weight_grads(h):
        rows = slice(h * HEAD, (h + 1) * HEAD)
        grad_weight[h % 2] = tn(vs[rows], gs[rows])

    def soften(h):
        weights = softmax_t(score[h % SLOTS])
        score[h % SLOTS] = weights
        weight_low[h % SLOTS] = weights.astype(BF16)

    def weigh(h):
        grad_score[h % 2] = score_grad(score[h % SLOTS], grad_weight[h % 2])

    def gather(h):
        rows = slice(h * HEAD, (h + 1) * HEAD)
        parts = (
            nn(ks[rows], grad_score[h % 2]) * SCALE,
            nt(qs[rows], grad_score[h % 2]) * SCALE,
            nt(gs[rows], weight_low[h % SLOTS]),
        )
        for kind, part in enumerate(parts):
            sgt[kind * CH + h * HEAD : kind * CH + (h + 1) * HEAD] = part.astype(BF16)

    loads[0].wait()
    loads[1].wait()
    for h in range(AHEAD):
        scores(h)
    loads[2].wait()
    loads[3].wait()
    for copy in loads[5:7]:
        copy.start()
    gs[...] = nt(wos[...], cot[...]).astype(BF16)
    for h in range(AHEAD):
        soften(h)
    lines_entered(line_sem.at[0])
    for copy in loads[7:]:
        copy.start()
    loads[4].wait()
    for step in range(HEADS + 2):
        if AHEAD <= step + 1 < HEADS:
            scores(step + 1)
        if step < HEADS:
            weight_grads(step)
        if AHEAD <= step < HEADS:
            soften(step)
        if 0 <= step - 1 < HEADS:
            weigh(step - 1)
        if 0 <= step - 2 < HEADS:
            gather(step - 2)
            done = (step - 1) * HEAD
            for block in range(0, 3 * CH, 128):
                stop = min(block + 128, 3 * CH)
                need = max(min(stop - kind * CH, CH) for kind in range(3) if block < (kind + 1) * CH and stop > kind * CH)
                if done - HEAD < need <= done:
                    sg[:, block:stop] = sgt[block:stop].T
    planes_entered(line_sem)
    loads[5].wait()

    for n in range(0, FEATURES, 256):
        cols = slice(n, min(n + 256, FEATURES))
        mid[:, cols] = (cot[:, cols].astype(F32) + nn(sg[...], w[:, cols])).astype(BF16)
    loads[6].wait()
    entered(line_sem.at[1])

    low = nt(mid[...], wot[0:256]).astype(BF16)
    stage1[0] = nn(e01[...], low[:, 0:128]).astype(BF16)
    stage1[1] = nn(e01[...], low[:, 128:256]).astype(BF16)
    stage1[2] = (nn(e20[...], low[:, 0:128]) + nn(e21[...], low[:, 128:256])).astype(BF16)
    send(stage1, recv1, send1, recv1_sem.at[0], *CHUNKS1[0])
    high = nt(mid[...], wot[256:576]).astype(BF16)
    stage1[3] = nn(e01[...], high[:, 0:128]).astype(BF16)
    stage1[4] = nn(e01[...], high[:, 128:256]).astype(BF16)
    stage1[5] = (nn(e20[...], high[:, 0:128]) + nn(e21[...], high[:, 128:256])).astype(BF16)
    rest = high[:, 256:320]
    stage1[6] = jnp.concatenate([nn(e01[...], rest), nn(e20[...], rest)], axis=1).astype(BF16)
    send(stage1, recv1, send1, recv1_sem.at[1], *CHUNKS1[1])

    for i in (7, 8, 9):
        loads[i].wait()

    def prepare(j, carry):
        for first in (0, 4):
            cuts = [slice(h * HEAD, (h + 1) * HEAD) for h in range(first, first + 4)]
            parts = [tn(kt[j, cut], qt[j, cut]) for cut in cuts]
            for i, part in enumerate(parts):
                pt[j, first + i] = softmax_t(part)
        return carry

    lax.fori_loop(0, POS, prepare, 0)

    def unpack1(base, c):
        for i in range(2):
            block = tn(recv1[base + i], weave[...]).astype(BF16)
            rows = slice((c + i) * 128, (c + i + 1) * 128)
            gt[0, rows] = block[:, :128]
            gt[1, rows] = block[:, 128:]
        block = tn(recv1[base + 2], weave[...]).astype(BF16)
        gt[2, c * 128 : (c + 1) * 128] = block[:, :128]
        gt[2, (c + 1) * 128 : (c + 2) * 128] = block[:, 128:]

    def temporal(lo, hi):
        def body(j, carry):
            heads = range(lo, hi)
            cuts = [slice(h * HEAD, (h + 1) * HEAD) for h in heads]
            weights = [pt[j, h] for h in heads]
            grads = [tn(vt[j, cut], gt[j, cut]) for cut in cuts]
            values = [nt(gt[j, cut], w.astype(BF16)) for cut, w in zip(cuts, weights)]
            scores = [score_grad(w, g) for w, g in zip(weights, grads)]
            queries = [nn(kt[j, cut], g) * SCALE for cut, g in zip(cuts, scores)]
            keys = [nt(qt[j, cut], g) * SCALE for cut, g in zip(cuts, scores)]
            size = (hi - lo) * HEAD
            for kind, parts in enumerate((queries, keys, values)):
                start = 3 * lo * HEAD + kind * size
                rt[j, start : start + size] = jnp.concatenate(parts, axis=0).astype(BF16)
            return carry

        lax.fori_loop(0, POS, body, 0)

    def pack2(t, c):
        wide = min(128, 3 * CH - (c + 1) * 128)
        for i, width in ((0, 128), (1, wide)):
            rows = slice((c + i) * 128, (c + i) * 128 + width)
            both = jnp.concatenate([rt[0, rows], rt[1, rows]], axis=1)
            stage2[t + i, :, 0:width] = nt(weave[...], both).astype(BF16)
        first = nt(weave[:, :128], rt[2, c * 128 : (c + 1) * 128])
        second = nt(weave[:, 128:], rt[2, (c + 1) * 128 : (c + 1) * 128 + wide])
        if wide < 128:
            second = jnp.concatenate([second, jnp.zeros((2 * FRAMES, 128 - wide), F32)], axis=1)
        stage2[t + 2] = (first + second).astype(BF16)

    def exchange(g):
        temporal(*GROUPS[g])
        lo, hi = CHUNKS2[g]
        for t in range(lo, hi, 3):
            pack2(t, t // 3 * 2)
        send(stage2, recv2, send2, recv2_sem.at[g], lo, hi)

    arrived(recv1, recv1_sem.at[0], *CHUNKS1[0])
    unpack1(0, 0)
    exchange(0)
    arrived(recv1, recv1_sem.at[1], *CHUNKS1[1])
    unpack1(3, 2)
    block = tn(recv1[6], weave[...]).astype(BF16)
    gt[0, 512:576] = block[:64, :128]
    gt[1, 512:576] = block[:64, 128:]
    gt[2, 512:576] = block[64:, :128]
    for g in range(1, len(GROUPS)):
        exchange(g)

    for g, (lo, hi) in enumerate(CHUNKS2):
        arrived(recv2, recv2_sem.at[g], lo, hi)
        if lo < LAST:
            unpack2(recv2, e01, e20, e21, part, lo, hi)
    sent(stage1, send1)
    sent(stage2, send2)


def finish(mid, recv, picked, part, mid_o, out_o, out, mid_sem, out_sem):
    keep = pltpu.make_async_copy(mid, mid_o, mid_sem)
    keep.start()
    stores = []

    def store(src, kind, lo, hi):
        rows = pl.ds(kind * CH + lo, hi - lo)
        copy = pltpu.make_async_copy(src.at[rows], out_o.at[rows], out_sem.at[len(stores)])
        copy.start()
        stores.append(copy)

    for kind in range(3):
        store(part, kind, 0, SPLIT[kind])
    unpack2(recv, *(picked.at[i] for i in range(3)), out, LAST, SLOTS2)
    for kind in range(3):
        store(out, kind, SPLIT[kind], CH)
    keep.wait()
    for copy in stores:
        copy.wait()


def local(cot, wos, wqkv, wot, qs, ks, vs, qt, kt, vt):
    def flip(a):
        return a[0].T

    def turn(a):
        return jnp.transpose(a, (1, 2, 0))

    hbm = pl.BlockSpec(memory_space=pl.ANY)
    vmem = pl.BlockSpec(memory_space=pltpu.VMEM)
    spatial = pltpu.VMEM((CH, TOKENS), BF16)
    temporal = pltpu.VMEM((POS, CH, FRAMES), BF16)
    middle, blocks, picked, part = pl.pallas_call(
        kernel,
        out_shape=(
            pltpu.VMEM((TOKENS, FEATURES), BF16),
            pltpu.VMEM((SLOTS2, 2 * FRAMES, 128), BF16),
            pltpu.VMEM((3, 2 * FRAMES, TOKENS), BF16),
            pltpu.VMEM((3 * CH, TOKENS), BF16),
        ),
        in_specs=[hbm] * 10,
        out_specs=(vmem, vmem, vmem, vmem),
        scratch_shapes=[
            pltpu.VMEM((TOKENS, FEATURES), BF16),
            pltpu.VMEM((CH, FEATURES), BF16),
            pltpu.VMEM((3 * CH, FEATURES), BF16),
            pltpu.VMEM((CH, FEATURES), BF16),
            spatial, spatial, spatial,
            temporal, temporal, temporal,
            spatial,
            pltpu.VMEM((3 * CH, TOKENS), BF16),
            pltpu.VMEM((TOKENS, 3 * CH), BF16),
            pltpu.VMEM((POS, HEADS, FRAMES, FRAMES), F32),
            temporal,
            pltpu.VMEM((POS, 3 * CH, FRAMES), BF16),
            pltpu.VMEM((2 * FRAMES, 2 * FRAMES), BF16),
            pltpu.VMEM((SLOTS, TOKENS, TOKENS), F32),
            pltpu.VMEM((2, TOKENS, TOKENS), F32),
            pltpu.VMEM((SLOTS, TOKENS, TOKENS), BF16),
            pltpu.VMEM((2, TOKENS, TOKENS), BF16),
            pltpu.VMEM((SLOTS1, 2 * FRAMES, 128), BF16),
            pltpu.VMEM((SLOTS1, 2 * FRAMES, 128), BF16),
            pltpu.VMEM((SLOTS2, 2 * FRAMES, 128), BF16),
            pltpu.SemaphoreType.DMA((10,)),
            pltpu.SemaphoreType.DMA,
            pltpu.SemaphoreType.DMA((len(CHUNKS1),)),
            pltpu.SemaphoreType.DMA,
            pltpu.SemaphoreType.DMA((len(CHUNKS2),)),
            pltpu.SemaphoreType.REGULAR((2,)),
        ],
        compiler_params=pltpu.CompilerParams(
            collective_id=0, has_side_effects=True, vmem_limit_bytes=56 << 20
        ),
        name="reward_backward",
    )(
        cot[0], wos, wqkv.T, wot,
        flip(qs), flip(ks), flip(vs),
        turn(qt), turn(kt), turn(vt),
    )
    middle, grads = pl.pallas_call(
        finish,
        out_shape=(
            jax.ShapeDtypeStruct((TOKENS, FEATURES), BF16),
            jax.ShapeDtypeStruct((3 * CH, TOKENS), BF16),
        ),
        in_specs=[vmem] * 4,
        out_specs=(hbm, hbm),
        scratch_shapes=[
            pltpu.VMEM((3 * CH, TOKENS), BF16),
            pltpu.SemaphoreType.DMA,
            pltpu.SemaphoreType.DMA((6,)),
        ],
        compiler_params=pltpu.CompilerParams(vmem_limit_bytes=16 << 20),
        name="unpack",
    )(middle, blocks, picked, part)
    return middle[None], grads.T[None]


def solution(mesh):
    frames = P(("sample", "outer", "inner"), None, None)
    positions = P("sample", ("outer", "inner"), None)
    return jax.shard_map(
        local,
        mesh=mesh,
        in_specs=(frames, P(), P(), P(), frames, frames, frames, positions, positions, positions),
        out_specs=(frames, frames),
        check_vma=False,
    )
```

```python
import functools

import jax
import jax.numpy as jnp
from jax import lax
from jax.experimental import pallas as pl
from jax.experimental.pallas import tpu as pltpu
from jax.sharding import PartitionSpec as P

HEADS = 8
HEAD = 72
CH = HEADS * HEAD
GROUPS = ((0, 3), (3, 6), (6, 8))
TOKENS = 384
FRAMES = 128
POS = 3
FEATURES = 1152
SLOTS = 4
AHEAD = 3
SLOTS1 = 7
SLOTS2 = 21
CHUNKS1 = ((0, 3), (3, 7))
CHUNKS2 = ((0, 6), (6, 15), (15, 21))
LAST = CHUNKS2[-1][0]
SPLIT = (432, 432, 416)
SCALE = HEAD ** -0.5
LOG2E = 1.4426950408889634
F32 = jnp.float32
BF16 = jnp.bfloat16


def dot(a, b, ca, cb):
    return lax.dot_general(a, b, (((ca,), (cb,)), ((), ())), preferred_element_type=F32)


def nn(a, b):
    return dot(a, b, 1, 0)


def nt(a, b):
    return dot(a, b, 1, 1)


def tn(a, b):
    return dot(a, b, 0, 0)


def coords():
    outer, inner = lax.axis_index("outer"), lax.axis_index("inner")
    y = outer * 2 + lax.div(inner, 32)
    z = lax.rem(lax.div(inner, 4), 8)
    x = lax.rem(inner, 4)
    return y, z, x


def device(y, z, x):
    return lax.axis_index("sample") * FRAMES + (y * 8 + z) * 4 + x


def my_index():
    return lax.axis_index("outer") * 64 + lax.axis_index("inner")


def greet(sem, line):
    y, z, x = coords()
    if line == "x":
        peers = [(y, z, lax.rem(x + i, 4)) for i in range(1, 4)]
    elif line == "y":
        peers = [(lax.rem(y + i, 4), z, x) for i in range(1, 4)]
    else:
        peers = [(y, lax.rem(z + i, 8), x) for i in range(1, 8)]
    for peer in peers:
        pl.semaphore_signal(
            sem, inc=1, device_id=device(*peer), device_id_type=pl.DeviceIdType.LOGICAL
        )


def enter():
    barrier = pltpu.get_barrier_semaphore()
    for line in "zyx":
        greet(barrier, line)


def lines_entered(sem):
    pl.semaphore_wait(pltpu.get_barrier_semaphore(), 13)
    greet(sem, "x")


def planes_entered(sems):
    pl.semaphore_wait(sems.at[0], 3)
    greet(sems.at[1], "y")


def entered(sem):
    pl.semaphore_wait(sem, 3)


def send(stage, recv, send_sem, recv_sem, lo, hi):
    me = my_index()
    sample = lax.axis_index("sample")
    y, z, x = coords()
    sign = 1 - 2 * sample
    depth = [lax.rem(z + sign * i + 8, 8) * 4 for i in range(8)]
    land = recv.at[lo:hi, pl.ds(pl.multiple_of(me * 2, 2), 2)]
    pltpu.make_async_copy(stage.at[lo:hi, pl.ds(pl.multiple_of(me * 2, 2), 2)], land, recv_sem).start()

    def one(across, away):
        ty = lax.rem(y + sign * lax.div(across, 4) + 4, 4)
        tx = lax.rem(x + sign * lax.rem(across, 4) + 4, 4)
        index = ty * 32 + depth[away] + tx
        pltpu.make_async_remote_copy(
            src_ref=stage.at[lo:hi, pl.ds(pl.multiple_of(index * 2, 2), 2)],
            dst_ref=land,
            send_sem=send_sem,
            recv_sem=recv_sem,
            device_id=sample * FRAMES + index,
            device_id_type=pl.DeviceIdType.LOGICAL,
        ).start()

    def body(turn, carry):
        for i, away in enumerate((4, 1, 7, 2, 6, 3, 5)):
            one(lax.rem(turn + 5 * i + 5, 16), away)
        one(turn + 1, 0)
        return carry

    lax.fori_loop(0, 15, body, 0)
    for i, away in enumerate((4, 1, 7, 2, 6, 3, 5)):
        one((15 + 5 * i + 5) % 16, away)


def arrived(recv, sem, lo, hi):
    pltpu.make_async_copy(recv.at[lo:hi], recv.at[lo:hi], sem).wait()


def sent(stage, sem):
    part = stage.at[:, : 2 * (FRAMES - 1)]
    pltpu.make_async_copy(part, part, sem).wait()


def softmax_t(scores):
    top = jnp.max(scores, axis=0, keepdims=True)
    weights = jnp.exp2((scores - top) * (SCALE * LOG2E))
    return weights * (1.0 / jnp.sum(weights, axis=0, keepdims=True))


def score_grad(weights, grad_weight):
    inner = jnp.sum(weights * grad_weight, axis=0, keepdims=True)
    return (weights * (grad_weight - inner)).astype(BF16)


def unpack2(recv, e01, e20, e21, out, lo, hi):
    def put(c, block):
        at, stop = c * 128, c * 128 + block.shape[0]
        for first, last in GROUPS:
            size = (last - first) * HEAD
            for kind in range(3):
                start = 3 * first * HEAD + kind * size
                a, b = max(at, start), min(stop, start + size)
                if a < b:
                    dest = kind * CH + first * HEAD + a - start
                    out[dest : dest + b - a] = block[a - at : b - at]

    for t in range(lo, hi, 3):
        c = t // 3 * 2
        wide = min(128, 3 * CH - (c + 1) * 128)
        pair = recv[t + 2]
        put(c, (tn(recv[t], e01[...]) + tn(pair, e20[...])).astype(BF16))
        last = (tn(recv[t + 1], e01[...]) + tn(pair, e21[...])).astype(BF16)
        put(c + 1, last[:wide])


def picks(e01, e20, e21):
    row = lax.broadcasted_iota(jnp.int32, (2 * FRAMES, TOKENS), 0)
    col = lax.broadcasted_iota(jnp.int32, (2 * FRAMES, TOKENS), 1)
    half, index = row & 1, row >> 1
    e01[...] = (col == 3 * index + half).astype(F32).astype(BF16)
    e20[...] = ((col == 3 * index + 2) & (half == 0)).astype(F32).astype(BF16)
    e21[...] = ((col == 3 * index + 2) & (half == 1)).astype(F32).astype(BF16)


def kernel(
    cot_h, wos_h, w_h, wot_h, qs_h, ks_h, vs_h, qt_h, kt_h, vt_h,
    mid, recv2, picked, part,
    cot, wos, w, wot, qs, ks, vs, qt, kt, vt,
    gs, sgt, sg, pt, gt, rt, weave,
    score, grad_weight, weight_low, grad_score, stage1, recv1, stage2,
    in_sem, send1, recv1_sem, send2, recv2_sem, line_sem,
):
    loads = []
    order = ((qs_h, qs), (ks_h, ks), (cot_h, cot), (wos_h, wos), (vs_h, vs), (w_h, w), (wot_h, wot), (qt_h, qt), (kt_h, kt), (vt_h, vt))
    for i, (src, dst) in enumerate(order):
        loads.append(pltpu.make_async_copy(src, dst, in_sem.at[i]))
    for copy in loads[:5]:
        copy.start()
    enter()

    e01, e20, e21 = (picked.at[i] for i in range(3))
    picks(e01, e20, e21)
    row = lax.broadcasted_iota(jnp.int32, (2 * FRAMES, 2 * FRAMES), 0)
    col = lax.broadcasted_iota(jnp.int32, (2 * FRAMES, 2 * FRAMES), 1)
    weave[...] = (col == (row & 1) * FRAMES + (row >> 1)).astype(F32).astype(BF16)

    def scores(h):
        rows = slice(h * HEAD, (h + 1) * HEAD)
        score[h % SLOTS] = tn(ks[rows], qs[rows])

    def weight_grads(h):
        rows = slice(h * HEAD, (h + 1) * HEAD)
        grad_weight[h % 2] = tn(vs[rows], gs[rows])

    def soften(h):
        weights = softmax_t(score[h % SLOTS])
        score[h % SLOTS] = weights
        weight_low[h % SLOTS] = weights.astype(BF16)

    def weigh(h):
        grad_score[h % 2] = score_grad(score[h % SLOTS], grad_weight[h % 2])

    def gather(h):
        rows = slice(h * HEAD, (h + 1) * HEAD)
        sgt[rows] = (nn(ks[rows], grad_score[h % 2]) * SCALE).astype(BF16)
        sg[:, CH + h * HEAD : CH + (h + 1) * HEAD] = (nt(grad_score[h % 2], qs[rows]) * SCALE).astype(BF16)
        sg[:, 2 * CH + h * HEAD : 2 * CH + (h + 1) * HEAD] = nt(weight_low[h % SLOTS], gs[rows]).astype(BF16)

    loads[0].wait()
    loads[1].wait()
    for h in range(AHEAD):
        scores(h)
    loads[2].wait()
    loads[3].wait()
    for copy in loads[5:7]:
        copy.start()
    gs[...] = nt(wos[...], cot[...]).astype(BF16)
    for h in range(AHEAD):
        soften(h)
    lines_entered(line_sem.at[0])
    for copy in loads[7:]:
        copy.start()
    loads[4].wait()
    for step in range(HEADS + 2):
        if AHEAD <= step + 1 < HEADS:
            scores(step + 1)
        if step < HEADS:
            weight_grads(step)
        if AHEAD <= step < HEADS:
            soften(step)
        if 0 <= step - 1 < HEADS:
            weigh(step - 1)
        if 0 <= step - 2 < HEADS:
            gather(step - 2)
            done = (step - 1) * HEAD
            for block in range(0, CH, 128):
                stop = min(block + 128, CH)
                if done - HEAD < stop <= done:
                    sg[:, block:stop] = sgt[block:stop].T
    planes_entered(line_sem)
    loads[5].wait()

    for n in range(0, FEATURES, 256):
        cols = slice(n, min(n + 256, FEATURES))
        mid[:, cols] = (cot[:, cols].astype(F32) + nn(sg[...], w[:, cols])).astype(BF16)
    loads[6].wait()
    entered(line_sem.at[1])

    low = nt(mid[...], wot[0:256]).astype(BF16)
    stage1[0] = nn(e01[...], low[:, 0:128]).astype(BF16)
    stage1[1] = nn(e01[...], low[:, 128:256]).astype(BF16)
    stage1[2] = (nn(e20[...], low[:, 0:128]) + nn(e21[...], low[:, 128:256])).astype(BF16)
    send(stage1, recv1, send1, recv1_sem.at[0], *CHUNKS1[0])
    high = nt(mid[...], wot[256:576]).astype(BF16)
    stage1[3] = nn(e01[...], high[:, 0:128]).astype(BF16)
    stage1[4] = nn(e01[...], high[:, 128:256]).astype(BF16)
    stage1[5] = (nn(e20[...], high[:, 0:128]) + nn(e21[...], high[:, 128:256])).astype(BF16)
    rest = high[:, 256:320]
    stage1[6] = jnp.concatenate([nn(e01[...], rest), nn(e20[...], rest)], axis=1).astype(BF16)
    send(stage1, recv1, send1, recv1_sem.at[1], *CHUNKS1[1])

    for i in (7, 8, 9):
        loads[i].wait()

    def prepare(j, carry):
        for first in (0, 4):
            cuts = [slice(h * HEAD, (h + 1) * HEAD) for h in range(first, first + 4)]
            parts = [tn(kt[j, cut], qt[j, cut]) for cut in cuts]
            for i, part in enumerate(parts):
                pt[j, first + i] = softmax_t(part)
        return carry

    lax.fori_loop(0, POS, prepare, 0)

    def unpack1(base, c):
        for i in range(2):
            block = tn(recv1[base + i], weave[...]).astype(BF16)
            rows = slice((c + i) * 128, (c + i + 1) * 128)
            gt[0, rows] = block[:, :128]
            gt[1, rows] = block[:, 128:]
        block = tn(recv1[base + 2], weave[...]).astype(BF16)
        gt[2, c * 128 : (c + 1) * 128] = block[:, :128]
        gt[2, (c + 1) * 128 : (c + 2) * 128] = block[:, 128:]

    def temporal(lo, hi):
        def body(j, carry):
            heads = range(lo, hi)
            cuts = [slice(h * HEAD, (h + 1) * HEAD) for h in heads]
            weights = [pt[j, h] for h in heads]
            grads = [tn(vt[j, cut], gt[j, cut]) for cut in cuts]
            values = [nt(gt[j, cut], w.astype(BF16)) for cut, w in zip(cuts, weights)]
            scores = [score_grad(w, g) for w, g in zip(weights, grads)]
            queries = [nn(kt[j, cut], g) * SCALE for cut, g in zip(cuts, scores)]
            keys = [nt(qt[j, cut], g) * SCALE for cut, g in zip(cuts, scores)]
            size = (hi - lo) * HEAD
            for kind, parts in enumerate((queries, keys, values)):
                start = 3 * lo * HEAD + kind * size
                rt[j, start : start + size] = jnp.concatenate(parts, axis=0).astype(BF16)
            return carry

        lax.fori_loop(0, POS, body, 0)

    def pack2(t, c):
        wide = min(128, 3 * CH - (c + 1) * 128)
        for i, width in ((0, 128), (1, wide)):
            rows = slice((c + i) * 128, (c + i) * 128 + width)
            both = jnp.concatenate([rt[0, rows], rt[1, rows]], axis=1)
            stage2[t + i, :, 0:width] = nt(weave[...], both).astype(BF16)
        first = nt(weave[:, :128], rt[2, c * 128 : (c + 1) * 128])
        second = nt(weave[:, 128:], rt[2, (c + 1) * 128 : (c + 1) * 128 + wide])
        if wide < 128:
            second = jnp.concatenate([second, jnp.zeros((2 * FRAMES, 128 - wide), F32)], axis=1)
        stage2[t + 2] = (first + second).astype(BF16)

    def exchange(g):
        temporal(*GROUPS[g])
        lo, hi = CHUNKS2[g]
        for t in range(lo, hi, 3):
            pack2(t, t // 3 * 2)
        send(stage2, recv2, send2, recv2_sem.at[g], lo, hi)

    arrived(recv1, recv1_sem.at[0], *CHUNKS1[0])
    unpack1(0, 0)
    exchange(0)
    arrived(recv1, recv1_sem.at[1], *CHUNKS1[1])
    unpack1(3, 2)
    block = tn(recv1[6], weave[...]).astype(BF16)
    gt[0, 512:576] = block[:64, :128]
    gt[1, 512:576] = block[:64, 128:]
    gt[2, 512:576] = block[64:, :128]
    for g in range(1, len(GROUPS)):
        exchange(g)

    for g, (lo, hi) in enumerate(CHUNKS2):
        arrived(recv2, recv2_sem.at[g], lo, hi)
        if lo < LAST:
            unpack2(recv2, e01, e20, e21, part, lo, hi)
    sent(stage1, send1)
    sent(stage2, send2)


def finish(mid, recv, picked, part, mid_o, out_o, out, mid_sem, out_sem):
    keep = pltpu.make_async_copy(mid, mid_o, mid_sem)
    keep.start()
    stores = []

    def store(src, kind, lo, hi):
        rows = pl.ds(kind * CH + lo, hi - lo)
        copy = pltpu.make_async_copy(src.at[rows], out_o.at[rows], out_sem.at[len(stores)])
        copy.start()
        stores.append(copy)

    for kind in range(3):
        store(part, kind, 0, SPLIT[kind])
    unpack2(recv, *(picked.at[i] for i in range(3)), out, LAST, SLOTS2)
    for kind in range(3):
        store(out, kind, SPLIT[kind], CH)
    keep.wait()
    for copy in stores:
        copy.wait()


def local(cot, wos, wqkv, wot, qs, ks, vs, qt, kt, vt):
    def flip(a):
        return a[0].T

    def turn(a):
        return jnp.transpose(a, (1, 2, 0))

    hbm = pl.BlockSpec(memory_space=pl.ANY)
    vmem = pl.BlockSpec(memory_space=pltpu.VMEM)
    spatial = pltpu.VMEM((CH, TOKENS), BF16)
    temporal = pltpu.VMEM((POS, CH, FRAMES), BF16)
    middle, blocks, picked, part = pl.pallas_call(
        kernel,
        out_shape=(
            pltpu.VMEM((TOKENS, FEATURES), BF16),
            pltpu.VMEM((SLOTS2, 2 * FRAMES, 128), BF16),
            pltpu.VMEM((3, 2 * FRAMES, TOKENS), BF16),
            pltpu.VMEM((3 * CH, TOKENS), BF16),
        ),
        in_specs=[hbm] * 10,
        out_specs=(vmem, vmem, vmem, vmem),
        scratch_shapes=[
            pltpu.VMEM((TOKENS, FEATURES), BF16),
            pltpu.VMEM((CH, FEATURES), BF16),
            pltpu.VMEM((3 * CH, FEATURES), BF16),
            pltpu.VMEM((CH, FEATURES), BF16),
            spatial, spatial, spatial,
            temporal, temporal, temporal,
            spatial,
            spatial,
            pltpu.VMEM((TOKENS, 3 * CH), BF16),
            pltpu.VMEM((POS, HEADS, FRAMES, FRAMES), F32),
            temporal,
            pltpu.VMEM((POS, 3 * CH, FRAMES), BF16),
            pltpu.VMEM((2 * FRAMES, 2 * FRAMES), BF16),
            pltpu.VMEM((SLOTS, TOKENS, TOKENS), F32),
            pltpu.VMEM((2, TOKENS, TOKENS), F32),
            pltpu.VMEM((SLOTS, TOKENS, TOKENS), BF16),
            pltpu.VMEM((2, TOKENS, TOKENS), BF16),
            pltpu.VMEM((SLOTS1, 2 * FRAMES, 128), BF16),
            pltpu.VMEM((SLOTS1, 2 * FRAMES, 128), BF16),
            pltpu.VMEM((SLOTS2, 2 * FRAMES, 128), BF16),
            pltpu.SemaphoreType.DMA((10,)),
            pltpu.SemaphoreType.DMA,
            pltpu.SemaphoreType.DMA((len(CHUNKS1),)),
            pltpu.SemaphoreType.DMA,
            pltpu.SemaphoreType.DMA((len(CHUNKS2),)),
            pltpu.SemaphoreType.REGULAR((2,)),
        ],
        compiler_params=pltpu.CompilerParams(
            collective_id=0, has_side_effects=True, vmem_limit_bytes=56 << 20
        ),
        name="reward_backward",
    )(
        cot[0], wos, wqkv.T, wot,
        flip(qs), flip(ks), flip(vs),
        turn(qt), turn(kt), turn(vt),
    )
    middle, grads = pl.pallas_call(
        finish,
        out_shape=(
            jax.ShapeDtypeStruct((TOKENS, FEATURES), BF16),
            jax.ShapeDtypeStruct((3 * CH, TOKENS), BF16),
        ),
        in_specs=[vmem] * 4,
        out_specs=(hbm, hbm),
        scratch_shapes=[
            pltpu.VMEM((3 * CH, TOKENS), BF16),
            pltpu.SemaphoreType.DMA,
            pltpu.SemaphoreType.DMA((6,)),
        ],
        compiler_params=pltpu.CompilerParams(vmem_limit_bytes=16 << 20),
        name="unpack",
    )(middle, blocks, picked, part)
    return middle[None], grads.T[None]


def solution(mesh):
    frames = P(("sample", "outer", "inner"), None, None)
    positions = P("sample", ("outer", "inner"), None)
    return jax.shard_map(
        local,
        mesh=mesh,
        in_specs=(frames, P(), P(), P(), frames, frames, frames, positions, positions, positions),
        out_specs=(frames, frames),
        check_vma=False,
    )
```

```python
import functools

import jax
import jax.numpy as jnp
from jax import lax
from jax.experimental import pallas as pl
from jax.experimental.pallas import tpu as pltpu
from jax.sharding import PartitionSpec as P

HEADS = 8
HEAD = 72
CH = HEADS * HEAD
GROUPS = ((0, 3), (3, 6), (6, 8))
TOKENS = 384
FRAMES = 128
POS = 3
FEATURES = 1152
SLOTS = 4
AHEAD = 3
SLOTS1 = 7
SLOTS2 = 21
CHUNKS1 = ((0, 3), (3, 7))
CHUNKS2 = ((0, 6), (6, 15), (15, 21))
LAST = CHUNKS2[-1][0]
SPLIT = (432, 432, 416)
SCALE = HEAD ** -0.5
LOG2E = 1.4426950408889634
F32 = jnp.float32
BF16 = jnp.bfloat16


def dot(a, b, ca, cb):
    return lax.dot_general(a, b, (((ca,), (cb,)), ((), ())), preferred_element_type=F32)


def nn(a, b):
    return dot(a, b, 1, 0)


def nt(a, b):
    return dot(a, b, 1, 1)


def tn(a, b):
    return dot(a, b, 0, 0)


def coords():
    outer, inner = lax.axis_index("outer"), lax.axis_index("inner")
    y = outer * 2 + lax.div(inner, 32)
    z = lax.rem(lax.div(inner, 4), 8)
    x = lax.rem(inner, 4)
    return y, z, x


def device(y, z, x):
    return lax.axis_index("sample") * FRAMES + (y * 8 + z) * 4 + x


def my_index():
    return lax.axis_index("outer") * 64 + lax.axis_index("inner")


def greet(sem, line):
    y, z, x = coords()
    if line == "x":
        peers = [(y, z, lax.rem(x + i, 4)) for i in range(1, 4)]
    elif line == "y":
        peers = [(lax.rem(y + i, 4), z, x) for i in range(1, 4)]
    else:
        peers = [(y, lax.rem(z + i, 8), x) for i in range(1, 8)]
    for peer in peers:
        pl.semaphore_signal(
            sem, inc=1, device_id=device(*peer), device_id_type=pl.DeviceIdType.LOGICAL
        )


def enter():
    barrier = pltpu.get_barrier_semaphore()
    for line in "zyx":
        greet(barrier, line)


def lines_entered(sem):
    pl.semaphore_wait(pltpu.get_barrier_semaphore(), 13)
    greet(sem, "x")


def planes_entered(sems):
    pl.semaphore_wait(sems.at[0], 3)
    greet(sems.at[1], "y")


def entered(sem):
    pl.semaphore_wait(sem, 3)


def send(stage, recv, send_sem, recv_sem, lo, hi):
    me = my_index()
    sample = lax.axis_index("sample")
    y, z, x = coords()
    sign = 1 - 2 * sample
    depth = [lax.rem(z + sign * i + 8, 8) * 4 for i in range(8)]
    land = recv.at[lo:hi, pl.ds(pl.multiple_of(me * 2, 2), 2)]
    pltpu.make_async_copy(stage.at[lo:hi, pl.ds(pl.multiple_of(me * 2, 2), 2)], land, recv_sem).start()

    def one(across, away):
        ty = lax.rem(y + sign * lax.div(across, 4) + 4, 4)
        tx = lax.rem(x + sign * lax.rem(across, 4) + 4, 4)
        index = ty * 32 + depth[away] + tx
        pltpu.make_async_remote_copy(
            src_ref=stage.at[lo:hi, pl.ds(pl.multiple_of(index * 2, 2), 2)],
            dst_ref=land,
            send_sem=send_sem,
            recv_sem=recv_sem,
            device_id=sample * FRAMES + index,
            device_id_type=pl.DeviceIdType.LOGICAL,
        ).start()

    def body(turn, carry):
        for i, away in enumerate((4, 1, 7, 2, 6, 3, 5)):
            one(lax.rem(turn + 5 * i + 5, 16), away)
        one(turn + 1, 0)
        return carry

    lax.fori_loop(0, 15, body, 0)
    for i, away in enumerate((4, 1, 7, 2, 6, 3, 5)):
        one((15 + 5 * i + 5) % 16, away)


def arrived(recv, sem, lo, hi):
    pltpu.make_async_copy(recv.at[lo:hi], recv.at[lo:hi], sem).wait()


def sent(stage, sem):
    part = stage.at[:, : 2 * (FRAMES - 1)]
    pltpu.make_async_copy(part, part, sem).wait()


def softmax_t(scores):
    top = jnp.max(scores, axis=0, keepdims=True)
    weights = jnp.exp2((scores - top) * (SCALE * LOG2E))
    return weights * (1.0 / jnp.sum(weights, axis=0, keepdims=True))


def score_grad(weights, grad_weight):
    inner = jnp.sum(weights * grad_weight, axis=0, keepdims=True)
    return (weights * (grad_weight - inner)).astype(BF16)


def unpack2(recv, e01, e20, e21, out, lo, hi):
    def put(c, block):
        at, stop = c * 128, c * 128 + block.shape[0]
        for first, last in GROUPS:
            size = (last - first) * HEAD
            for kind in range(3):
                start = 3 * first * HEAD + kind * size
                a, b = max(at, start), min(stop, start + size)
                if a < b:
                    dest = kind * CH + first * HEAD + a - start
                    out[dest : dest + b - a] = block[a - at : b - at]

    for t in range(lo, hi, 3):
        c = t // 3 * 2
        wide = min(128, 3 * CH - (c + 1) * 128)
        pair = recv[t + 2]
        put(c, (tn(recv[t], e01[...]) + tn(pair, e20[...])).astype(BF16))
        last = (tn(recv[t + 1], e01[...]) + tn(pair, e21[...])).astype(BF16)
        put(c + 1, last[:wide])


def picks(e01, e20, e21):
    row = lax.broadcasted_iota(jnp.int32, (2 * FRAMES, TOKENS), 0)
    col = lax.broadcasted_iota(jnp.int32, (2 * FRAMES, TOKENS), 1)
    half, index = row & 1, row >> 1
    e01[...] = (col == 3 * index + half).astype(F32).astype(BF16)
    e20[...] = ((col == 3 * index + 2) & (half == 0)).astype(F32).astype(BF16)
    e21[...] = ((col == 3 * index + 2) & (half == 1)).astype(F32).astype(BF16)


def kernel(
    cot_h, wos_h, w_h, wot_h, qs_h, ks_h, vs_h, qt_h, kt_h, vt_h,
    mid, recv2, picked, part,
    cot, wos, w, wot, qs, ks, vs, qt, kt, vt,
    gs, sgt, sg, pt, gt, rt, weave,
    score, grad_weight, weight_low, grad_score, stage1, recv1, stage2,
    in_sem, send1, recv1_sem, send2, recv2_sem, line_sem,
):
    loads = []
    order = ((qs_h, qs), (ks_h, ks), (cot_h, cot), (wos_h, wos), (vs_h, vs), (w_h, w), (wot_h, wot), (qt_h, qt), (kt_h, kt), (vt_h, vt))
    for i, (src, dst) in enumerate(order):
        loads.append(pltpu.make_async_copy(src, dst, in_sem.at[i]))
    for copy in loads[:5]:
        copy.start()
    enter()

    e01, e20, e21 = (picked.at[i] for i in range(3))
    picks(e01, e20, e21)
    row = lax.broadcasted_iota(jnp.int32, (2 * FRAMES, 2 * FRAMES), 0)
    col = lax.broadcasted_iota(jnp.int32, (2 * FRAMES, 2 * FRAMES), 1)
    weave[...] = (col == (row & 1) * FRAMES + (row >> 1)).astype(F32).astype(BF16)

    def scores(h):
        rows = slice(h * HEAD, (h + 1) * HEAD)
        score[h % SLOTS] = tn(ks[rows], qs[rows])

    def weight_grads(h):
        rows = slice(h * HEAD, (h + 1) * HEAD)
        grad_weight[h % 2] = tn(vs[rows], gs[rows])

    def soften(h):
        weights = softmax_t(score[h % SLOTS])
        score[h % SLOTS] = weights
        weight_low[h % SLOTS] = weights.astype(BF16)

    def weigh(h):
        grad_score[h % 2] = score_grad(score[h % SLOTS], grad_weight[h % 2])

    def gather(h):
        rows = slice(h * HEAD, (h + 1) * HEAD)
        sgt[rows] = (nn(ks[rows], grad_score[h % 2]) * SCALE).astype(BF16)
        sg[:, CH + h * HEAD : CH + (h + 1) * HEAD] = (nt(grad_score[h % 2], qs[rows]) * SCALE).astype(BF16)
        sg[:, 2 * CH + h * HEAD : 2 * CH + (h + 1) * HEAD] = nt(weight_low[h % SLOTS], gs[rows]).astype(BF16)

    loads[0].wait()
    loads[1].wait()
    for h in range(AHEAD):
        scores(h)
    loads[2].wait()
    loads[3].wait()
    for copy in loads[5:7]:
        copy.start()
    gs[...] = nt(wos[...], cot[...]).astype(BF16)
    for h in range(AHEAD):
        soften(h)
    lines_entered(line_sem.at[0])
    for copy in loads[7:]:
        copy.start()
    loads[4].wait()
    for step in range(HEADS + 2):
        if AHEAD <= step + 1 < HEADS:
            scores(step + 1)
        if step < HEADS:
            weight_grads(step)
        if AHEAD <= step < HEADS:
            soften(step)
        if 0 <= step - 1 < HEADS:
            weigh(step - 1)
        if 0 <= step - 2 < HEADS:
            gather(step - 2)
            done = (step - 1) * HEAD
            for block in range(0, CH, 128):
                stop = min(block + 128, CH)
                if done - HEAD < stop <= done:
                    sg[:, block:stop] = sgt[block:stop].T
    planes_entered(line_sem)
    loads[5].wait()

    for n in range(0, FEATURES, 256):
        cols = slice(n, min(n + 256, FEATURES))
        mid[:, cols] = (cot[:, cols].astype(F32) + nn(sg[...], w[:, cols])).astype(BF16)
    loads[6].wait()
    entered(line_sem.at[1])

    low = nt(mid[...], wot[0:256]).astype(BF16)
    both = nn(e01[...], low).astype(BF16)
    stage1[0] = both[:, :128]
    stage1[1] = both[:, 128:]
    stage1[2] = (nn(e20[...], low[:, 0:128]) + nn(e21[...], low[:, 128:256])).astype(BF16)
    send(stage1, recv1, send1, recv1_sem.at[0], *CHUNKS1[0])
    high = nt(mid[...], wot[256:576]).astype(BF16)
    stage1[3] = nn(e01[...], high[:, 0:128]).astype(BF16)
    stage1[4] = nn(e01[...], high[:, 128:256]).astype(BF16)
    stage1[5] = (nn(e20[...], high[:, 0:128]) + nn(e21[...], high[:, 128:256])).astype(BF16)
    rest = high[:, 256:320]
    stage1[6] = jnp.concatenate([nn(e01[...], rest), nn(e20[...], rest)], axis=1).astype(BF16)
    send(stage1, recv1, send1, recv1_sem.at[1], *CHUNKS1[1])

    for i in (7, 8, 9):
        loads[i].wait()

    def prepare(j, carry):
        for first in (0, 4):
            cuts = [slice(h * HEAD, (h + 1) * HEAD) for h in range(first, first + 4)]
            parts = [tn(kt[j, cut], qt[j, cut]) for cut in cuts]
            for i, part in enumerate(parts):
                pt[j, first + i] = softmax_t(part)
        return carry

    lax.fori_loop(0, POS, prepare, 0)

    def unpack1(base, c):
        for i in range(2):
            block = tn(recv1[base + i], weave[...]).astype(BF16)
            rows = slice((c + i) * 128, (c + i + 1) * 128)
            gt[0, rows] = block[:, :128]
            gt[1, rows] = block[:, 128:]
        block = tn(recv1[base + 2], weave[...]).astype(BF16)
        gt[2, c * 128 : (c + 1) * 128] = block[:, :128]
        gt[2, (c + 1) * 128 : (c + 2) * 128] = block[:, 128:]

    def temporal(lo, hi):
        def body(j, carry):
            heads = range(lo, hi)
            cuts = [slice(h * HEAD, (h + 1) * HEAD) for h in heads]
            weights = [pt[j, h] for h in heads]
            grads = [tn(vt[j, cut], gt[j, cut]) for cut in cuts]
            values = [nt(gt[j, cut], w.astype(BF16)) for cut, w in zip(cuts, weights)]
            scores = [score_grad(w, g) for w, g in zip(weights, grads)]
            queries = [nn(kt[j, cut], g) * SCALE for cut, g in zip(cuts, scores)]
            keys = [nt(qt[j, cut], g) * SCALE for cut, g in zip(cuts, scores)]
            size = (hi - lo) * HEAD
            for kind, parts in enumerate((queries, keys, values)):
                start = 3 * lo * HEAD + kind * size
                rt[j, start : start + size] = jnp.concatenate(parts, axis=0).astype(BF16)
            return carry

        lax.fori_loop(0, POS, body, 0)

    def pack2(t, c):
        wide = min(128, 3 * CH - (c + 1) * 128)
        for i, width in ((0, 128), (1, wide)):
            rows = slice((c + i) * 128, (c + i) * 128 + width)
            both = jnp.concatenate([rt[0, rows], rt[1, rows]], axis=1)
            stage2[t + i, :, 0:width] = nt(weave[...], both).astype(BF16)
        first = nt(weave[:, :128], rt[2, c * 128 : (c + 1) * 128])
        second = nt(weave[:, 128:], rt[2, (c + 1) * 128 : (c + 1) * 128 + wide])
        if wide < 128:
            second = jnp.concatenate([second, jnp.zeros((2 * FRAMES, 128 - wide), F32)], axis=1)
        stage2[t + 2] = (first + second).astype(BF16)

    def exchange(g):
        temporal(*GROUPS[g])
        lo, hi = CHUNKS2[g]
        for t in range(lo, hi, 3):
            pack2(t, t // 3 * 2)
        send(stage2, recv2, send2, recv2_sem.at[g], lo, hi)

    arrived(recv1, recv1_sem.at[0], *CHUNKS1[0])
    unpack1(0, 0)
    exchange(0)
    arrived(recv1, recv1_sem.at[1], *CHUNKS1[1])
    unpack1(3, 2)
    block = tn(recv1[6], weave[...]).astype(BF16)
    gt[0, 512:576] = block[:64, :128]
    gt[1, 512:576] = block[:64, 128:]
    gt[2, 512:576] = block[64:, :128]
    for g in range(1, len(GROUPS)):
        exchange(g)

    for g, (lo, hi) in enumerate(CHUNKS2):
        arrived(recv2, recv2_sem.at[g], lo, hi)
        if lo < LAST:
            unpack2(recv2, e01, e20, e21, part, lo, hi)
    sent(stage1, send1)
    sent(stage2, send2)


def finish(mid, recv, picked, part, mid_o, out_o, out, mid_sem, out_sem):
    keep = pltpu.make_async_copy(mid, mid_o, mid_sem)
    keep.start()
    stores = []

    def store(src, kind, lo, hi):
        rows = pl.ds(kind * CH + lo, hi - lo)
        copy = pltpu.make_async_copy(src.at[rows], out_o.at[rows], out_sem.at[len(stores)])
        copy.start()
        stores.append(copy)

    for kind in range(3):
        store(part, kind, 0, SPLIT[kind])
    unpack2(recv, *(picked.at[i] for i in range(3)), out, LAST, SLOTS2)
    for kind in range(3):
        store(out, kind, SPLIT[kind], CH)
    keep.wait()
    for copy in stores:
        copy.wait()


def local(cot, wos, wqkv, wot, qs, ks, vs, qt, kt, vt):
    def flip(a):
        return a[0].T

    def turn(a):
        return jnp.transpose(a, (1, 2, 0))

    hbm = pl.BlockSpec(memory_space=pl.ANY)
    vmem = pl.BlockSpec(memory_space=pltpu.VMEM)
    spatial = pltpu.VMEM((CH, TOKENS), BF16)
    temporal = pltpu.VMEM((POS, CH, FRAMES), BF16)
    middle, blocks, picked, part = pl.pallas_call(
        kernel,
        out_shape=(
            pltpu.VMEM((TOKENS, FEATURES), BF16),
            pltpu.VMEM((SLOTS2, 2 * FRAMES, 128), BF16),
            pltpu.VMEM((3, 2 * FRAMES, TOKENS), BF16),
            pltpu.VMEM((3 * CH, TOKENS), BF16),
        ),
        in_specs=[hbm] * 10,
        out_specs=(vmem, vmem, vmem, vmem),
        scratch_shapes=[
            pltpu.VMEM((TOKENS, FEATURES), BF16),
            pltpu.VMEM((CH, FEATURES), BF16),
            pltpu.VMEM((3 * CH, FEATURES), BF16),
            pltpu.VMEM((CH, FEATURES), BF16),
            spatial, spatial, spatial,
            temporal, temporal, temporal,
            spatial,
            spatial,
            pltpu.VMEM((TOKENS, 3 * CH), BF16),
            pltpu.VMEM((POS, HEADS, FRAMES, FRAMES), F32),
            temporal,
            pltpu.VMEM((POS, 3 * CH, FRAMES), BF16),
            pltpu.VMEM((2 * FRAMES, 2 * FRAMES), BF16),
            pltpu.VMEM((SLOTS, TOKENS, TOKENS), F32),
            pltpu.VMEM((2, TOKENS, TOKENS), F32),
            pltpu.VMEM((SLOTS, TOKENS, TOKENS), BF16),
            pltpu.VMEM((2, TOKENS, TOKENS), BF16),
            pltpu.VMEM((SLOTS1, 2 * FRAMES, 128), BF16),
            pltpu.VMEM((SLOTS1, 2 * FRAMES, 128), BF16),
            pltpu.VMEM((SLOTS2, 2 * FRAMES, 128), BF16),
            pltpu.SemaphoreType.DMA((10,)),
            pltpu.SemaphoreType.DMA,
            pltpu.SemaphoreType.DMA((len(CHUNKS1),)),
            pltpu.SemaphoreType.DMA,
            pltpu.SemaphoreType.DMA((len(CHUNKS2),)),
            pltpu.SemaphoreType.REGULAR((2,)),
        ],
        compiler_params=pltpu.CompilerParams(
            collective_id=0, has_side_effects=True, vmem_limit_bytes=56 << 20
        ),
        name="reward_backward",
    )(
        cot[0], wos, wqkv.T, wot,
        flip(qs), flip(ks), flip(vs),
        turn(qt), turn(kt), turn(vt),
    )
    middle, grads = pl.pallas_call(
        finish,
        out_shape=(
            jax.ShapeDtypeStruct((TOKENS, FEATURES), BF16),
            jax.ShapeDtypeStruct((3 * CH, TOKENS), BF16),
        ),
        in_specs=[vmem] * 4,
        out_specs=(hbm, hbm),
        scratch_shapes=[
            pltpu.VMEM((3 * CH, TOKENS), BF16),
            pltpu.SemaphoreType.DMA,
            pltpu.SemaphoreType.DMA((6,)),
        ],
        compiler_params=pltpu.CompilerParams(vmem_limit_bytes=16 << 20),
        name="unpack",
    )(middle, blocks, picked, part)
    return middle[None], grads.T[None]


def solution(mesh):
    frames = P(("sample", "outer", "inner"), None, None)
    positions = P("sample", ("outer", "inner"), None)
    return jax.shard_map(
        local,
        mesh=mesh,
        in_specs=(frames, P(), P(), P(), frames, frames, frames, positions, positions, positions),
        out_specs=(frames, frames),
        check_vma=False,
    )
```
